256 devices in a mesh: row: 32 (over x_lo, z, core), col: 8 (over x_hi, y).
Axes of the slice: x: 4 (x_hi: 2, x_lo: 2; x = x_hi * 2 + x_lo), y: 4, z: 8, core: 2. Of those that a mesh axis runs over, the one named last changes fastest.
Arguments:
- ham: bfloat16 [8192, 8192], P('row'), may hold values from -0.2 to 1.7, as said below
- coeff: bfloat16 [8192, 8192], P('row', 'col'), may hold values from -40 to 40, as said below
- tile_mask: int32 [256, 256], P('row'), may hold values from 0 to 1, as said below
- occupation: int32 [16, 8192], replicated, may hold values from 0 to 1, as said below
- orbital_energy: float32 [16], replicated, may hold values from -0.4 to 0.6
- coulomb: float32 [16, 16], replicated, may hold values from 0.005 to 0.04
Outputs:
- correction: float32 [8192, 8192], P('row', 'col')
- stats: float32 [2], replicated
The draws below stay inside these ranges and needn't reach their ends.
Inputs may be any that keep to these rules, and one draw needn't show every extreme that they name: ham is symmetric. coeff is symmetric. tile_mask is symmetric with ones on its diagonal. `occupation`: every column holds exactly 6 ones.
All inputs are finite; a program needn't handle non-finite values.
Results may differ from the reference program's by a relative error of at most 0.0003.
Values may be sent and summed in bfloat16 or wider, within the bound.
No kernel may reach another device: no remote copies, remote signals or barrier semaphores. Data moves between devices by JAX's collectives and lax.ppermute only.
A program may use at most 128 MiB of HBM per device.

```python
import math
import jax
import jax.numpy as jnp
from jax import lax

NS = 8192
NORB = 16
NEL = 6
STR_BLOCK = 32


def string_scales(key):
    uniform_part = jax.random.uniform(key, (NS,), jnp.float32)
    position = jnp.arange(NS, dtype=jnp.float32) / NS
    return jnp.exp(uniform_part * math.log(10.0)) * (1.0 + position)


def draw_coeff(key, part):
    key_entries = jax.random.fold_in(key, 11)
    key_scales = jax.random.fold_in(key, 12)
    entries = jax.random.normal(key_entries, (NS, NS), jnp.float32)
    scales = string_scales(key_scales)
    norm_scale = 50.0
    paired = jnp.clip((entries + entries.T) * 0.7071, -4.0, 4.0)
    return (paired * scales[:, None] * scales[None, :] / norm_scale).astype(jnp.bfloat16)


def draw_ham(key, part):
    key_entries = jax.random.fold_in(key, 21)
    key_diagonal = jax.random.fold_in(key, 22)
    entries = jnp.clip(jax.random.normal(key_entries, (NS, NS), jnp.float32), -6.0, 6.0)
    diagonal = jax.random.uniform(key_diagonal, (NS,), jnp.float32, 0.5, 1.5)
    paired = (entries + entries.T) * (0.7071 / math.sqrt(NS))
    return (paired + jnp.diag(diagonal)).astype(jnp.bfloat16)


def draw_tile_mask(key, part):
    block_count = NS // STR_BLOCK
    coin_flips = jax.random.randint(jax.random.fold_in(key, 31), (block_count, block_count), 0, 2, jnp.int32)
    row_index = jnp.arange(block_count, dtype=jnp.int32)[:, None]
    col_index = jnp.arange(block_count, dtype=jnp.int32)[None, :]
    mirrored = jnp.where(row_index <= col_index, coin_flips, coin_flips.T)
    return jnp.where(row_index == col_index, 1, mirrored).astype(jnp.int32)


def draw_occupation(key, part):
    keys_all = jax.random.split(jax.random.fold_in(key, 41), NS)
    orders = jax.vmap(lambda one_key: jax.random.permutation(one_key, NORB))(keys_all)
    return (orders < NEL).astype(jnp.int32).T


def setup_inputs(seed: int = 0) -> dict:
    arg_keys = jax.random.split(jax.random.key(seed), 7)
    return {
        "ham": draw_ham(jax.random.fold_in(arg_keys[6], 71), 0),
        "coeff": draw_coeff(jax.random.fold_in(arg_keys[6], 71), 0),
        "tile_mask": draw_tile_mask(jax.random.fold_in(arg_keys[6], 71), 0),
        "occupation": draw_occupation(jax.random.fold_in(arg_keys[6], 71), 0),
        "orbital_energy": jnp.clip(jax.random.uniform(arg_keys[4], (NORB,), jnp.float32, -0.4, 0.6), -0.4, 0.6),
        "coulomb": jnp.clip(jnp.exp(jax.random.uniform(arg_keys[5], (NORB, NORB), jnp.float32, math.log(0.005), math.log(0.04))), 0.005, 0.04),
    }


def reference(ham, coeff, tile_mask, occupation, orbital_energy, coulomb):
    block_count = tile_mask.shape[0]
    block_size = NS // block_count
    weights = tile_mask.astype(jnp.bfloat16)[:, None, :, None]
    masked = (ham.reshape(block_count, block_size, block_count, block_size) * weights).reshape(NS, NS)
    product = jnp.dot(masked, coeff, preferred_element_type=jnp.float32)
    sigma = product + product.T
    coeff_float = coeff.astype(jnp.float32)
    theta = jnp.sum(coeff_float * sigma) / jnp.sum(coeff_float * coeff_float)
    occ_float = occupation.astype(jnp.float32)
    energy = jnp.dot(orbital_energy, occ_float, precision=lax.Precision.HIGHEST)
    coupling = jnp.dot(jnp.dot(occ_float.T, coulomb, precision=lax.Precision.HIGHEST), occ_float, precision=lax.Precision.HIGHEST)
    diagonal = energy[:, None] + energy[None, :] + coupling
    residual = sigma - theta * coeff_float
    update = residual / jnp.maximum(jnp.abs(diagonal - theta), 1.0)
    squares = jnp.sum(residual * residual)
    spread = jnp.sum(update * update)
    correction = update * lax.rsqrt(spread / (NS * NS) + 1e-06)
    stats = jnp.stack([theta, jnp.sqrt(squares / (NS * NS))])
    return (correction, stats)
```

```python
import jax
import jax.numpy as jnp
from jax import lax
from jax.experimental import pallas as pl
from jax.experimental.pallas import tpu as pltpu
from jax.sharding import Mesh, PartitionSpec as P

NS = 8192
AXES = ("xlo", "z", "core", "xhi", "y")
SIZES = (2, 8, 2, 2, 4)
ROW = ("xlo", "z", "core")
COL = ("xhi", "y")
LANES = 128


def mask_kernel(own_ref, pair_ref, mask_own_ref, mask_pair_ref, out_ref):
    rows, cols = own_ref.shape
    mask_rows, mask_cols = mask_own_ref.shape
    size = cols // mask_cols
    tile = rows // mask_rows
    spread = (
        lax.broadcasted_iota(jnp.int32, (mask_cols, cols), 1) // size
        == lax.broadcasted_iota(jnp.int32, (mask_cols, cols), 0)
    ).astype(jnp.bfloat16)
    for panel, (ham_ref, mask_ref) in enumerate(
        ((own_ref, mask_own_ref), (pair_ref, mask_pair_ref))
    ):
        mask = mask_ref[...].astype(jnp.float32).astype(jnp.bfloat16)
        wide = jnp.dot(mask, spread, preferred_element_type=jnp.float32)
        for index in range(mask_rows):
            at = index * tile
            values = ham_ref[at : at + tile, :].astype(jnp.float32) * wide[index : index + 1, :]
            out_ref[panel * rows + at : panel * rows + at + tile, :] = values.astype(jnp.bfloat16)


def mask_panels(own, pair, mask_own, mask_pair):
    rows, cols = own.shape
    mask_rows, mask_cols = mask_own.shape
    parts = 2
    width = cols // parts
    ham_spec = pl.BlockSpec((rows, width), lambda j: (0, j))
    mask_spec = pl.BlockSpec((mask_rows, mask_cols // parts), lambda j: (0, j))
    return pl.pallas_call(
        mask_kernel,
        grid=(parts,),
        in_specs=[ham_spec, ham_spec, mask_spec, mask_spec],
        out_specs=pl.BlockSpec((2 * rows, width), lambda j: (0, j)),
        out_shape=jax.ShapeDtypeStruct((2 * rows, cols), jnp.bfloat16),
        compiler_params=pltpu.CompilerParams(vmem_limit_bytes=48 * 1024 * 1024),
        cost_estimate=pl.CostEstimate(
            flops=2 * rows * cols, bytes_accessed=8 * rows * cols, transcendentals=0
        ),
    )(own, pair, mask_own, mask_pair)


def swap(value, axis):
    return lax.ppermute(value, axis, [(0, 1), (1, 0)])


def shift(value, step):
    count = lax.axis_size("z")
    return lax.ppermute(value, "z", [(i, (i + step) % count) for i in range(count)])


def exchange(value, axes):
    return lax.all_to_all(value, axes, split_axis=0, concat_axis=0, tiled=True)


def scalar_tile(first, second):
    lane = lax.broadcasted_iota(jnp.int32, (8, LANES), 1)
    row = lax.broadcasted_iota(jnp.int32, (8, LANES), 0)
    return jnp.where(
        row == 0, jnp.where(lane == 0, first, jnp.where(lane == 1, second, 0.0)), 0.0
    )


def gather_blocks(block):
    near = {0: block}
    far = {}
    near[-1], near[1], far[0] = shift(near[0], 1), shift(near[0], -1), swap(near[0], "xlo")
    near[-2], near[2], far[-1] = shift(near[-1], 1), shift(near[1], -1), swap(near[-1], "xlo")
    near[-3], near[3], far[1] = shift(near[-2], 1), shift(near[2], -1), swap(near[1], "xlo")
    near[-4], far[2], far[-2] = shift(near[-3], 1), shift(far[1], -1), swap(near[-2], "xlo")
    far[-3], far[3], far[-4] = shift(far[-2], 1), shift(far[2], -1), swap(near[-4], "xlo")
    order = [(0, 0), (0, -1), (0, 1), (1, 0), (0, -2), (0, 2), (1, -1), (0, -3), (0, 3), (1, 1)]
    order += [(0, -4), (1, 2), (1, -2), (1, -3), (1, 3), (1, -4)]
    return [(side, offset, (far if side else near)[offset]) for side, offset in order]


def body(ham, coeff, tile_mask, occupation, orbital_energy, coulomb):
    rows, strings = ham.shape
    cols = coeff.shape[1]
    half = cols // 2
    core = lax.axis_index("core")
    xlo = lax.axis_index("xlo")
    z = lax.axis_index("z")
    row_index = (xlo * 8 + z) * 2 + core
    col_index = lax.axis_index("xhi") * 4 + lax.axis_index("y")

    first = core == 0
    left, right = coeff[:, :half], coeff[:, half:]
    mine = jnp.where(first, left, right)
    theirs = swap(jnp.where(first, right, left), "core")
    block = jnp.where(
        first,
        jnp.concatenate([mine, theirs], axis=0),
        jnp.concatenate([theirs, mine], axis=0),
    )
    panels = mask_panels(ham, swap(ham, "core"), tile_mask, swap(tile_mask, "core"))
    depth = block.shape[0]

    product = None
    for side, offset, piece in gather_blocks(block):
        owner = (xlo + side) % 2 * 8 + (z + offset) % 8
        columns = lax.dynamic_slice_in_dim(panels, owner * depth, depth, 1)
        term = jnp.dot(columns, piece, preferred_element_type=jnp.float32)
        product = term if product is None else product + term
    kept, sent = product[:rows], product[rows:]
    got = swap(sent, "core")
    product = jnp.where(
        first,
        jnp.concatenate([kept, got], axis=1),
        jnp.concatenate([got, kept], axis=1),
    )

    coeff_float = coeff.astype(jnp.float32)
    sums = scalar_tile(2.0 * jnp.sum(coeff_float * product), jnp.sum(coeff_float * coeff_float))

    sub = rows // 8
    pieces = product.reshape(8, sub, 8, LANES).transpose(0, 2, 1, 3).reshape(8, rows, LANES)
    pieces = jnp.concatenate([pieces, jnp.broadcast_to(sums, (8, 8, LANES))], axis=1)
    pieces = exchange(pieces, COL)
    sums = jnp.sum(pieces[:, rows:], axis=0)
    pieces = pieces[:, :rows].reshape(32, 2 * sub, LANES)
    pieces = jnp.concatenate([pieces, jnp.broadcast_to(sums, (32, 8, LANES))], axis=1)
    pieces = exchange(pieces, ROW)
    sums = jnp.sum(pieces[:, 2 * sub :], axis=0)
    pieces = exchange(pieces[:, : 2 * sub].reshape(8, 4 * 2 * sub, LANES), COL)
    turned = pieces.reshape(8, 4, 2, sub, LANES).transpose(2, 4, 1, 0, 3).reshape(rows, cols)

    occ_float = occupation.astype(jnp.float32)
    occ_alpha = lax.dynamic_slice_in_dim(occ_float, row_index * rows, rows, 1)
    occ_beta = lax.dynamic_slice_in_dim(occ_float, col_index * cols, cols, 1)
    energy_alpha = jnp.dot(orbital_energy, occ_alpha, precision=lax.Precision.HIGHEST)
    energy_beta = jnp.dot(orbital_energy, occ_beta, precision=lax.Precision.HIGHEST)
    coupling = jnp.dot(
        jnp.dot(occ_alpha.T, coulomb, precision=lax.Precision.HIGHEST),
        occ_beta,
        precision=lax.Precision.HIGHEST,
    )
    diagonal = energy_alpha[:, None] + energy_beta[None, :] + coupling

    theta = sums[0, 0] / sums[0, 1]
    residual = product + turned - theta * coeff_float
    update = residual / jnp.maximum(jnp.abs(diagonal - theta), 1.0)
    totals = scalar_tile(jnp.sum(residual * residual), jnp.sum(update * update))[0]
    totals = jnp.sum(exchange(jnp.broadcast_to(totals, (256, LANES)), AXES), axis=0)
    correction = update * lax.rsqrt(totals[1] / (NS * NS) + 1e-06)
    stats = jnp.stack([theta, jnp.sqrt(totals[0] / (NS * NS))])
    return (correction, stats)


def solution(mesh):
    fine = Mesh(mesh.devices.reshape(SIZES), AXES)
    in_specs = (P(ROW, None), P(ROW, COL), P(ROW, None), P(), P(), P())
    out_specs = (P(ROW, COL), P())
    return jax.shard_map(body, mesh=fine, in_specs=in_specs, out_specs=out_specs, check_vma=False)
```

```python
import jax
import jax.numpy as jnp
from jax import lax
from jax.experimental import pallas as pl
from jax.experimental.pallas import tpu as pltpu
from jax.sharding import Mesh, PartitionSpec as P

NS = 8192
AXES = ("xlo", "z", "core", "xhi", "y")
SIZES = (2, 8, 2, 2, 4)
ROW = ("xlo", "z", "core")
COL = ("xhi", "y")
PLANE = ("xlo", "core", "xhi", "y")
LANES = 128
CHUNK = 1024
MIB = 1024 * 1024


def mask_kernel(ham_ref, mask_ref, out_ref):
    rows, cols = ham_ref.shape
    mask_rows, mask_cols = mask_ref.shape
    size = cols // mask_cols
    tile = rows // mask_rows
    spread = (
        lax.broadcasted_iota(jnp.int32, (mask_cols, cols), 1) // size
        == lax.broadcasted_iota(jnp.int32, (mask_cols, cols), 0)
    ).astype(jnp.bfloat16)
    mask = mask_ref[...].astype(jnp.float32).astype(jnp.bfloat16)
    wide = jnp.dot(mask, spread, preferred_element_type=jnp.float32)
    for index in range(mask_rows):
        at = index * tile
        values = ham_ref[at : at + tile, :].astype(jnp.float32) * wide[index : index + 1, :]
        out_ref[at : at + tile, :] = values.astype(jnp.bfloat16)


def mask_half(ham, tile_mask, half):
    rows, cols = ham.shape
    mask_rows, mask_cols = tile_mask.shape
    return pl.pallas_call(
        mask_kernel,
        grid=(1,),
        in_specs=[
            pl.BlockSpec((rows, cols // 2), lambda j: (0, half)),
            pl.BlockSpec((mask_rows, mask_cols // 2), lambda j: (0, half)),
        ],
        out_specs=pl.BlockSpec((rows, cols // 2), lambda j: (0, 0)),
        out_shape=jax.ShapeDtypeStruct((rows, cols // 2), jnp.bfloat16),
        compiler_params=pltpu.CompilerParams(vmem_limit_bytes=32 * MIB),
        cost_estimate=pl.CostEstimate(
            flops=rows * cols, bytes_accessed=2 * rows * cols, transcendentals=0
        ),
    )(ham, tile_mask)


def product_kernel(
    place_ref, c0, p1, p2, p3, m1, m2, m3, top, low,
    own_a, own_b, pair_a, pair_b, far_a, far_b, cross_a, cross_b,
    turn_ref, home_ref, lhs, acc, local,
):
    step = pl.program_id(0)
    steps = pl.num_programs(0)
    xlo, z, core = place_ref[0], place_ref[1], place_ref[2]

    for offset, ref in ((0, c0), (-1, p1), (-2, p2), (-3, p3), (1, m1), (2, m2), (3, m3)):
        at = pl.multiple_of(lax.rem(z + offset + 8, 8) * 32, 32)
        lhs[pl.ds(at, 32), :] = ref[...]
    at = pl.multiple_of(lax.rem(z + 4, 8) * 32, 32)
    lhs[pl.ds(at, 16), :] = top[...]
    lhs[pl.ds(pl.multiple_of(at + 16, 16), 16), :] = low[...]

    @pl.when(step == 0)
    def _():
        acc[...] = jnp.zeros_like(acc)

    def add(panels):
        for index, ref in enumerate(panels):
            side = xlo if index < 2 else 1 - xlo
            other = core if index % 2 == 0 else 1 - core
            columns = pl.ds(pl.multiple_of((side * 2 + other) * 256, 256), 256)
            acc[:, columns] += lax.dot_general(
                lhs[...], ref[...], (((1,), (1,)), ((), ())), preferred_element_type=jnp.float32
            )

    @pl.when(step < steps // 2)
    def _():
        add((own_a, pair_a, far_a, cross_a))

    @pl.when(step >= steps // 2)
    def _():
        add((own_b, pair_b, far_b, cross_b))

    for side in range(2):

        @pl.when(step == side * (steps // 2) + z // 2)
        def _():
            source = pl.ds(pl.multiple_of(lax.rem(z, 2) * 512, 512), 512)
            local[:, side * 512 : side * 512 + 512] = lhs[:, source]

    @pl.when(step == steps - 1)
    def _():
        coeff = local[...].astype(jnp.float32)
        projection = jnp.sum(2.0 * coeff * acc[...])
        weight = jnp.sum(coeff * coeff)
        lane = lax.broadcasted_iota(jnp.int32, (8, LANES), 1)
        row = lax.broadcasted_iota(jnp.int32, (8, LANES), 0)
        sums = jnp.where(lane == 0, projection, jnp.where(lane == 1, weight, 0.0))
        sums = jnp.where(row == 0, sums, 0.0)
        for there in range(8):
            for part in range(8):
                turn_ref[there, part * 32 : part * 32 + 32, :] = acc[
                    there * 32 : there * 32 + 32, part * LANES : part * LANES + LANES
                ]
            turn_ref[there, 256:264, :] = sums
        for target in range(32):
            quarter, col = target // 8, target % 8
            for part in range(2):
                lanes = quarter * 256 + part * LANES
                for below in range(2):
                    at = (2 * (col % 4) + below) * 32 + col // 4 * 16
                    home_ref[target, part * 32 + below * 16 : part * 32 + below * 16 + 16, :] = acc[
                        at : at + 16, lanes : lanes + LANES
                    ]


def multiply(place, blocks, halves):
    strings = blocks[0].shape[1]
    steps = strings // CHUNK
    half_steps = steps // 2
    block_specs = [pl.BlockSpec((b.shape[0], CHUNK), lambda j, place: (0, j)) for b in blocks]
    low_spec = pl.BlockSpec((256, CHUNK), lambda j, place: (0, jnp.minimum(j, half_steps - 1)))
    high_spec = pl.BlockSpec((256, CHUNK), lambda j, place: (0, jnp.maximum(j - half_steps, 0)))
    return pl.pallas_call(
        product_kernel,
        grid_spec=pltpu.PrefetchScalarGridSpec(
            num_scalar_prefetch=1,
            grid=(steps,),
            in_specs=block_specs + [low_spec, high_spec] * 4,
            out_specs=[
                pl.BlockSpec((8, 264, LANES), lambda j, place: (0, 0, 0)),
                pl.BlockSpec((32, 64, LANES), lambda j, place: (0, 0, 0)),
            ],
            scratch_shapes=[
                pltpu.VMEM((256, CHUNK), jnp.bfloat16),
                pltpu.VMEM((256, 1024), jnp.float32),
                pltpu.VMEM((256, 1024), jnp.bfloat16),
            ],
        ),
        out_shape=[
            jax.ShapeDtypeStruct((8, 264, LANES), jnp.float32),
            jax.ShapeDtypeStruct((32, 64, LANES), jnp.float32),
        ],
        compiler_params=pltpu.CompilerParams(vmem_limit_bytes=40 * MIB),
        cost_estimate=pl.CostEstimate(
            flops=2 * 256 * 1024 * strings, bytes_accessed=24 * MIB, transcendentals=0
        ),
    )(place, *blocks, *halves)


def update_kernel(home_ref, turn_ref, coeff_ref, diag_ref, update_ref, sums_ref):
    totals = jnp.sum(turn_ref[:, 64:72, :], axis=0)
    lane = lax.broadcasted_iota(jnp.int32, (8, LANES), 1)
    row = lax.broadcasted_iota(jnp.int32, (8, LANES), 0)
    projection = jnp.sum(jnp.where(lane == 0, totals, 0.0))
    weight = jnp.sum(jnp.where(lane == 1, totals, 0.0))
    theta = jnp.full((1, 1), projection) / jnp.full((1, 1), weight)
    squares = jnp.zeros((8, LANES), jnp.float32)
    spread = jnp.zeros((8, LANES), jnp.float32)
    for part in range(2):
        rows = slice(part * LANES, part * LANES + LANES)
        for index in range(8):
            cols = slice(index * LANES, index * LANES + LANES)
            quarter, group = index // 2, index % 2
            at = part * 32 + quarter * 8
            straight = home_ref[group * 16 : group * 16 + 16, at : at + 8, :]
            straight = straight.reshape(LANES, LANES).T
            turned = turn_ref[part * 16 : part * 16 + 16, index * 8 : index * 8 + 8, :]
            turned = turned.reshape(LANES, LANES)
            coeff = coeff_ref[rows, cols].astype(jnp.float32)
            residual = straight + turned - theta * coeff
            update = residual / jnp.maximum(jnp.abs(diag_ref[rows, cols] - theta), 1.0)
            update_ref[rows, cols] = update
            squares += jnp.sum((residual * residual).reshape(16, 8, LANES), axis=0)
            spread += jnp.sum((update * update).reshape(16, 8, LANES), axis=0)
    values = jnp.where(lane == 0, jnp.sum(squares), jnp.where(lane == 1, jnp.sum(spread), 0.0))
    values = jnp.where(lane == 2, theta, values)
    sums_ref[...] = jnp.where(row == 0, values, 0.0)


def make_update(home, turn, coeff, diagonal):
    return pl.pallas_call(
        update_kernel,
        out_shape=[
            jax.ShapeDtypeStruct(coeff.shape, jnp.float32),
            jax.ShapeDtypeStruct((8, LANES), jnp.float32),
        ],
        compiler_params=pltpu.CompilerParams(vmem_limit_bytes=32 * MIB),
        cost_estimate=pl.CostEstimate(
            flops=10 * coeff.size, bytes_accessed=5 * MIB, transcendentals=0
        ),
    )(home, turn, coeff, diagonal)


def swap(value):
    return lax.ppermute(value, "core", [(0, 1), (1, 0)])


def shift(value, step):
    count = lax.axis_size("z")
    return lax.ppermute(value, "z", [(i, (i + step) % count) for i in range(count)])


def shift_x(value, step):
    def index(x):
        return x % 2 * 2 + x // 2

    pairs = [(index(x), index((x + step) % 4)) for x in range(4)]
    return lax.ppermute(value, ("xlo", "xhi"), pairs)


def exchange(value, axes):
    return lax.all_to_all(value, axes, split_axis=0, concat_axis=0, tiled=True)


def body(ham, coeff, tile_mask, occupation, orbital_energy, coulomb):
    rows, strings = ham.shape
    cols = coeff.shape[1]
    core = lax.axis_index("core")
    xlo = lax.axis_index("xlo")
    z = lax.axis_index("z")
    row_index = (xlo * 8 + z) * 2 + core
    col_index = lax.axis_index("xhi") * 4 + lax.axis_index("y")

    own_a = mask_half(ham, tile_mask, 0)
    own_b = mask_half(ham, tile_mask, 1)
    far_a, far_b = shift_x(own_a, 1), shift_x(own_b, -1)
    pair_a, pair_b = swap(own_a), swap(own_b)
    cross_a, cross_b = swap(far_a), swap(far_b)

    coeff_in, own_a, own_b = lax.optimization_barrier((coeff, own_a, own_b))
    block = exchange(coeff_in.reshape(32, 8, cols), PLANE)
    block = block.reshape(4, 8, 8, cols).transpose(0, 2, 1, 3).reshape(32, strings)
    p1, m1 = shift(block, 1), shift(block, -1)
    p2, m2 = shift(p1, 1), shift(m1, -1)
    p3, m3 = shift(p2, 1), shift(m2, -1)
    top, low = shift(p3[:16], 1), shift(m3[16:], -1)

    place = jnp.stack([xlo, z, core]).astype(jnp.int32)
    turn, home = multiply(
        place,
        (block, p1, p2, p3, m1, m2, m3, top, low),
        (own_a, own_b, pair_a, pair_b, far_a, far_b, cross_a, cross_b),
    )

    home = exchange(home, PLANE)
    turn = exchange(turn, "z")
    sums = jnp.sum(turn[:, 256:], axis=0)
    turn = turn[:, :256].reshape(4, 2, 2, 2, 2, 2, 2, 8, LANES)
    turn = turn.transpose(5, 6, 2, 0, 1, 3, 4, 7, 8).reshape(32, 64, LANES)
    turn = jnp.concatenate([turn, jnp.broadcast_to(sums, (32, 8, LANES))], axis=1)
    turn = exchange(turn, PLANE)

    occ_float = occupation.astype(jnp.float32)
    occ_alpha = lax.dynamic_slice_in_dim(occ_float, row_index * rows, rows, 1)
    occ_beta = lax.dynamic_slice_in_dim(occ_float, col_index * cols, cols, 1)
    energy_alpha = jnp.dot(orbital_energy, occ_alpha, precision=lax.Precision.HIGHEST)
    energy_beta = jnp.dot(orbital_energy, occ_beta, precision=lax.Precision.HIGHEST)
    coupling = jnp.dot(
        jnp.dot(occ_alpha.T, coulomb, precision=lax.Precision.HIGHEST),
        occ_beta,
        precision=lax.Precision.HIGHEST,
    )
    diagonal = energy_alpha[:, None] + energy_beta[None, :] + coupling

    update, sums = make_update(home, turn, coeff, diagonal)
    theta = sums[0, 2]
    totals = exchange(jnp.broadcast_to(sums[0], (256, LANES)), AXES)
    totals = jnp.sum(totals, axis=0)
    correction = update * lax.rsqrt(totals[1] / (NS * NS) + 1e-06)
    stats = jnp.stack([theta, jnp.sqrt(totals[0] / (NS * NS))])
    return (correction, stats)


def solution(mesh):
    fine = Mesh(mesh.devices.reshape(SIZES), AXES)
    in_specs = (P(ROW, None), P(ROW, COL), P(ROW, None), P(), P(), P())
    out_specs = (P(ROW, COL), P())
    return jax.shard_map(body, mesh=fine, in_specs=in_specs, out_specs=out_specs, check_vma=False)
```

```python
import jax
import jax.numpy as jnp
from jax import lax
from jax.experimental import pallas as pl
from jax.experimental.pallas import tpu as pltpu
from jax.sharding import Mesh, PartitionSpec as P

NS = 8192
AXES = ("xlo", "z", "core", "xhi", "y")
SIZES = (2, 8, 2, 2, 4)
ROW = ("xlo", "z", "core")
COL = ("xhi", "y")
PLANE = ("xlo", "core", "xhi", "y")
LANES = 128
CHUNK = 1024
MIB = 1024 * 1024


def mask_kernel(ham_ref, mask_ref, out_ref):
    rows, cols = ham_ref.shape
    mask_rows, mask_cols = mask_ref.shape
    tile = size = rows // mask_rows
    spread = (
        lax.broadcasted_iota(jnp.int32, (mask_cols, cols), 1) // size + pl.program_id(0) * (cols // size)
        == lax.broadcasted_iota(jnp.int32, (mask_cols, cols), 0)
    ).astype(jnp.bfloat16)
    mask = mask_ref[...].astype(jnp.float32).astype(jnp.bfloat16)
    wide = jnp.dot(mask, spread, preferred_element_type=jnp.float32)
    for index in range(mask_rows):
        at = index * tile
        values = ham_ref[at : at + tile, :].astype(jnp.float32) * wide[index : index + 1, :]
        out_ref[at : at + tile, :] = values.astype(jnp.bfloat16)


def mask_half(ham, tile_mask, half):
    rows, cols = ham.shape
    mask_rows, mask_cols = tile_mask.shape
    return pl.pallas_call(
        mask_kernel,
        grid=(4,),
        in_specs=[
            pl.BlockSpec((rows, cols // 8), lambda j: (0, half * 4 + j)),
            pl.BlockSpec((mask_rows, mask_cols // 2), lambda j: (0, half)),
        ],
        out_specs=pl.BlockSpec((rows, cols // 8), lambda j: (0, j)),
        out_shape=jax.ShapeDtypeStruct((rows, cols // 2), jnp.bfloat16),
        compiler_params=pltpu.CompilerParams(vmem_limit_bytes=60 * MIB),
        cost_estimate=pl.CostEstimate(
            flops=rows * cols, bytes_accessed=2 * rows * cols, transcendentals=0
        ),
    )(ham, tile_mask)


def product_kernel(
    place_ref, c0, p1, p2, p3, m1, m2, m3, top, low,
    own_a, own_b, pair_a, pair_b, far_a, far_b, cross_a, cross_b,
    turn_ref, home_ref, lhs, acc, local,
):
    step = pl.program_id(0)
    steps = pl.num_programs(0)
    xlo, z, core = place_ref[0], place_ref[1], place_ref[2]

    for offset, ref in ((0, c0), (-1, p1), (-2, p2), (-3, p3), (1, m1), (2, m2), (3, m3)):
        at = pl.multiple_of(lax.rem(z + offset + 8, 8) * 32, 32)
        lhs[pl.ds(at, 32), :] = ref[...]
    at = pl.multiple_of(lax.rem(z + 4, 8) * 32, 32)
    lhs[pl.ds(at, 16), :] = top[...]
    lhs[pl.ds(pl.multiple_of(at + 16, 16), 16), :] = low[...]

    @pl.when(step == 0)
    def _():
        acc[...] = jnp.zeros_like(acc)

    def add(panels):
        for index, ref in enumerate(panels):
            side = xlo if index < 2 else 1 - xlo
            other = core if index % 2 == 0 else 1 - core
            columns = pl.ds(pl.multiple_of((side * 2 + other) * 256, 256), 256)
            acc[:, columns] += lax.dot_general(
                lhs[...], ref[...], (((1,), (1,)), ((), ())), preferred_element_type=jnp.float32
            )

    @pl.when(step < steps // 2)
    def _():
        add((own_a, pair_a, far_a, cross_a))

    @pl.when(step >= steps // 2)
    def _():
        add((own_b, pair_b, far_b, cross_b))

    for side in range(2):

        @pl.when(step == side * (steps // 2) + z // 2)
        def _():
            source = pl.ds(pl.multiple_of(lax.rem(z, 2) * 512, 512), 512)
            local[:, side * 512 : side * 512 + 512] = lhs[:, source]

    @pl.when(step == steps - 1)
    def _():
        coeff = local[...].astype(jnp.float32)
        projection = jnp.sum(2.0 * coeff * acc[...])
        weight = jnp.sum(coeff * coeff)
        lane = lax.broadcasted_iota(jnp.int32, (8, LANES), 1)
        row = lax.broadcasted_iota(jnp.int32, (8, LANES), 0)
        sums = jnp.where(lane == 0, projection, jnp.where(lane == 1, weight, 0.0))
        sums = jnp.where(row == 0, sums, 0.0)
        for there in range(8):
            for part in range(8):
                turn_ref[there, part * 32 : part * 32 + 32, :] = acc[
                    there * 32 : there * 32 + 32, part * LANES : part * LANES + LANES
                ]
            turn_ref[there, 256:264, :] = sums
        for target in range(32):
            quarter, col = target // 8, target % 8
            for part in range(2):
                lanes = quarter * 256 + part * LANES
                for below in range(2):
                    at = (2 * (col % 4) + below) * 32 + col // 4 * 16
                    home_ref[target, part * 32 + below * 16 : part * 32 + below * 16 + 16, :] = acc[
                        at : at + 16, lanes : lanes + LANES
                    ]


def multiply(place, blocks, halves):
    strings = blocks[0].shape[1]
    steps = strings // CHUNK
    half_steps = steps // 2
    block_specs = [pl.BlockSpec((b.shape[0], CHUNK), lambda j, place: (0, j)) for b in blocks]
    low_spec = pl.BlockSpec((256, CHUNK), lambda j, place: (0, jnp.minimum(j, half_steps - 1)))
    high_spec = pl.BlockSpec((256, CHUNK), lambda j, place: (0, jnp.maximum(j - half_steps, 0)))
    return pl.pallas_call(
        product_kernel,
        grid_spec=pltpu.PrefetchScalarGridSpec(
            num_scalar_prefetch=1,
            grid=(steps,),
            in_specs=block_specs + [low_spec, high_spec] * 4,
            out_specs=[
                pl.BlockSpec((8, 264, LANES), lambda j, place: (0, 0, 0)),
                pl.BlockSpec((32, 64, LANES), lambda j, place: (0, 0, 0)),
            ],
            scratch_shapes=[
                pltpu.VMEM((256, CHUNK), jnp.bfloat16),
                pltpu.VMEM((256, 1024), jnp.float32),
                pltpu.VMEM((256, 1024), jnp.bfloat16),
            ],
        ),
        out_shape=[
            jax.ShapeDtypeStruct((8, 264, LANES), jnp.float32),
            jax.ShapeDtypeStruct((32, 64, LANES), jnp.float32),
        ],
        compiler_params=pltpu.CompilerParams(vmem_limit_bytes=60 * MIB),
        cost_estimate=pl.CostEstimate(
            flops=2 * 256 * 1024 * strings, bytes_accessed=24 * MIB, transcendentals=0
        ),
    )(place, *blocks, *halves)


def update_kernel(tiles_ref, coeff_ref, diag_ref, update_ref, sums_ref):
    totals = jnp.sum(tiles_ref[:, 128:136, :], axis=0)
    lane = lax.broadcasted_iota(jnp.int32, (8, LANES), 1)
    row = lax.broadcasted_iota(jnp.int32, (8, LANES), 0)
    projection = jnp.sum(jnp.where(lane == 0, totals, 0.0))
    weight = jnp.sum(jnp.where(lane == 1, totals, 0.0))
    theta = jnp.full((1, 1), projection) / jnp.full((1, 1), weight)
    squares = jnp.zeros((8, LANES), jnp.float32)
    spread = jnp.zeros((8, LANES), jnp.float32)
    for part in range(2):
        rows = slice(part * LANES, part * LANES + LANES)
        for index in range(8):
            cols = slice(index * LANES, index * LANES + LANES)
            quarter, group = index // 2, index % 2
            at = part * 32 + quarter * 8
            straight = tiles_ref[group * 16 : group * 16 + 16, at : at + 8, :]
            straight = straight.reshape(LANES, LANES).T
            turned = tiles_ref[part * 16 : part * 16 + 16, 64 + index * 8 : 72 + index * 8, :]
            turned = turned.reshape(LANES, LANES)
            coeff = coeff_ref[rows, cols].astype(jnp.float32)
            residual = straight + turned - theta * coeff
            update = residual / jnp.maximum(jnp.abs(diag_ref[rows, cols] - theta), 1.0)
            update_ref[rows, cols] = update
            squares += jnp.sum((residual * residual).reshape(16, 8, LANES), axis=0)
            spread += jnp.sum((update * update).reshape(16, 8, LANES), axis=0)
    values = jnp.where(lane == 0, jnp.sum(squares), jnp.where(lane == 1, jnp.sum(spread), 0.0))
    values = jnp.where(lane == 2, theta, values)
    sums_ref[...] = jnp.where(row == 0, values, 0.0)


def make_update(tiles, coeff, diagonal):
    return pl.pallas_call(
        update_kernel,
        out_shape=[
            jax.ShapeDtypeStruct(coeff.shape, jnp.float32),
            jax.ShapeDtypeStruct((8, LANES), jnp.float32),
        ],
        compiler_params=pltpu.CompilerParams(vmem_limit_bytes=16 * MIB),
        cost_estimate=pl.CostEstimate(
            flops=10 * coeff.size, bytes_accessed=5 * MIB, transcendentals=0
        ),
    )(tiles, coeff, diagonal)


def swap(value):
    return lax.ppermute(value, "core", [(0, 1), (1, 0)])


def shift(value, step):
    count = lax.axis_size("z")
    return lax.ppermute(value, "z", [(i, (i + step) % count) for i in range(count)])


def shift_x(value, step):
    def index(x):
        return x % 2 * 2 + x // 2

    pairs = [(index(x), index((x + step) % 4)) for x in range(4)]
    return lax.ppermute(value, ("xlo", "xhi"), pairs)


def exchange(value, axes):
    return lax.all_to_all(value, axes, split_axis=0, concat_axis=0, tiled=True)


def body(ham, coeff, tile_mask, occupation, orbital_energy, coulomb):
    rows, strings = ham.shape
    cols = coeff.shape[1]
    core = lax.axis_index("core")
    xlo = lax.axis_index("xlo")
    z = lax.axis_index("z")
    row_index = (xlo * 8 + z) * 2 + core
    col_index = lax.axis_index("xhi") * 4 + lax.axis_index("y")

    own_a = mask_half(ham, tile_mask, 0)
    own_b = mask_half(ham, tile_mask, 1)
    pair_a, pair_b = swap(own_a), swap(own_b)

    block = exchange(coeff.reshape(32, 8, cols), PLANE)
    block, own_a, own_b, pair_a, pair_b = lax.optimization_barrier(
        (block, own_a, own_b, pair_a, pair_b)
    )
    far_a, far_b = shift_x(own_a, 1), shift_x(own_b, -1)
    block = block.reshape(4, 8, 8, cols).transpose(0, 2, 1, 3).reshape(32, strings)
    p1, m1 = lax.optimization_barrier((shift(block, 1), shift(block, -1)))
    p2, m2 = lax.optimization_barrier((shift(p1, 1), shift(m1, -1)))
    p3, m3, far_a, far_b = lax.optimization_barrier((shift(p2, 1), shift(m2, -1), far_a, far_b))
    cross_a, cross_b = swap(far_a), swap(far_b)
    top, low = shift(p3[:16], 1), shift(m3[16:], -1)

    place = jnp.stack([xlo, z, core]).astype(jnp.int32)
    turn, home = multiply(
        place,
        (block, p1, p2, p3, m1, m2, m3, top, low),
        (own_a, own_b, pair_a, pair_b, far_a, far_b, cross_a, cross_b),
    )

    turn = exchange(turn, "z")
    sums = jnp.sum(turn[:, 256:], axis=0)
    turn = turn[:, :256].reshape(4, 2, 2, 2, 2, 2, 2, 8, LANES)
    turn = turn.transpose(5, 6, 2, 0, 1, 3, 4, 7, 8).reshape(32, 64, LANES)
    tiles = jnp.concatenate([home, turn, jnp.broadcast_to(sums, (32, 8, LANES))], axis=1)
    tiles = exchange(tiles, PLANE)

    occ_float = occupation.astype(jnp.float32)
    occ_alpha = lax.dynamic_slice_in_dim(occ_float, row_index * rows, rows, 1)
    occ_beta = lax.dynamic_slice_in_dim(occ_float, col_index * cols, cols, 1)
    energy_alpha = jnp.dot(orbital_energy, occ_alpha, precision=lax.Precision.HIGHEST)
    energy_beta = jnp.dot(orbital_energy, occ_beta, precision=lax.Precision.HIGHEST)
    coupling = jnp.dot(
        jnp.dot(occ_alpha.T, coulomb, precision=lax.Precision.HIGHEST),
        occ_beta,
        precision=lax.Precision.HIGHEST,
    )
    diagonal = energy_alpha[:, None] + energy_beta[None, :] + coupling

    update, sums = make_update(tiles, coeff, diagonal)
    theta = sums[0, 2]
    totals = exchange(jnp.broadcast_to(sums[0], (256, LANES)), AXES)
    totals = jnp.sum(totals, axis=0)
    correction = update * lax.rsqrt(totals[1] / (NS * NS) + 1e-06)
    stats = jnp.stack([theta, jnp.sqrt(totals[0] / (NS * NS))])
    return (correction, stats)


def solution(mesh):
    fine = Mesh(mesh.devices.reshape(SIZES), AXES)
    in_specs = (P(ROW, None), P(ROW, COL), P(ROW, None), P(), P(), P())
    out_specs = (P(ROW, COL), P())
    return jax.shard_map(body, mesh=fine, in_specs=in_specs, out_specs=out_specs, check_vma=False)
```

```python
import functools

import jax
import jax.numpy as jnp
from jax import lax
from jax.experimental import pallas as pl
from jax.experimental.pallas import tpu as pltpu
from jax.sharding import Mesh, PartitionSpec as P

NS = 8192
AXES = ("xlo", "z", "core", "xhi", "y")
SIZES = (2, 8, 2, 2, 4)
ROW = ("xlo", "z", "core")
COL = ("xhi", "y")
PLANE = ("xlo", "core", "xhi", "y")
LANES = 128
CHUNK = 1024
MIB = 1024 * 1024


def mask_kernel(ham_ref, mask_ref, out_ref):
    rows, cols = ham_ref.shape
    mask_rows, mask_cols = mask_ref.shape
    tile = size = rows // mask_rows
    spread = (
        lax.broadcasted_iota(jnp.int32, (mask_cols, cols), 1) // size + pl.program_id(0) * (cols // size)
        == lax.broadcasted_iota(jnp.int32, (mask_cols, cols), 0)
    ).astype(jnp.bfloat16)
    mask = mask_ref[...].astype(jnp.float32).astype(jnp.bfloat16)
    wide = jnp.dot(mask, spread, preferred_element_type=jnp.float32)
    for index in range(mask_rows):
        at = index * tile
        values = ham_ref[at : at + tile, :].astype(jnp.float32) * wide[index : index + 1, :]
        out_ref[at : at + tile, :] = values.astype(jnp.bfloat16)


def mask_half(ham, tile_mask, half):
    rows, cols = ham.shape
    mask_rows, mask_cols = tile_mask.shape
    return pl.pallas_call(
        mask_kernel,
        grid=(4,),
        in_specs=[
            pl.BlockSpec((rows, cols // 8), lambda j: (0, half * 4 + j)),
            pl.BlockSpec((mask_rows, mask_cols // 2), lambda j: (0, half)),
        ],
        out_specs=pl.BlockSpec((rows, cols // 8), lambda j: (0, j)),
        out_shape=jax.ShapeDtypeStruct((rows, cols // 2), jnp.bfloat16),
        compiler_params=pltpu.CompilerParams(vmem_limit_bytes=8 * MIB),
        cost_estimate=pl.CostEstimate(
            flops=rows * cols, bytes_accessed=2 * rows * cols, transcendentals=0
        ),
    )(ham, tile_mask)


def product_kernel(
    place_ref, c0, p1, p2, p3, m1, m2, m3, top, low,
    own_a, own_b, pair_a, pair_b, far_a, far_b, cross_a, cross_b,
    turn_ref, home_ref, lhs, acc, local,
):
    xlo, z, core = place_ref[0], place_ref[1], place_ref[2]
    strings = c0.shape[1]
    blocks = ((0, c0), (-1, p1), (-2, p2), (-3, p3), (1, m1), (2, m2), (3, m3))
    acc[...] = jnp.zeros_like(acc)

    def gather(at, width, out):
        for offset, ref in blocks:
            row = pl.multiple_of(lax.rem(z + offset + 8, 8) * 32, 32)
            out[pl.ds(row, 32), :] = ref[:, pl.ds(at, width)]
        row = pl.multiple_of(lax.rem(z + 4, 8) * 32, 32)
        out[pl.ds(row, 16), :] = top[:, pl.ds(at, width)]
        out[pl.ds(pl.multiple_of(row + 16, 16), 16), :] = low[:, pl.ds(at, width)]

    for start, panels in (
        (0, (own_a, pair_a, far_a, cross_a)),
        (strings // 2, (own_b, pair_b, far_b, cross_b)),
    ):

        def step(index, carry, start=start, panels=panels):
            at = pl.multiple_of(index * CHUNK, CHUNK)
            gather(pl.multiple_of(start + at, CHUNK), CHUNK, lhs)
            for number, ref in enumerate(panels):
                side = xlo if number < 2 else 1 - xlo
                other = core if number % 2 == 0 else 1 - core
                columns = pl.ds(pl.multiple_of((side * 2 + other) * 256, 256), 256)
                acc[:, columns] += lax.dot_general(
                    lhs[...],
                    ref[:, pl.ds(at, CHUNK)],
                    (((1,), (1,)), ((), ())),
                    preferred_element_type=jnp.float32,
                )
            return carry

        lax.fori_loop(0, strings // 2 // CHUNK, step, 0)

    for side in range(2):
        at = pl.multiple_of(side * (strings // 2) + z * 512, 512)
        gather(at, 512, local.at[:, side * 512 : side * 512 + 512])

    coeff = local[...].astype(jnp.float32)
    projection = jnp.sum(2.0 * coeff * acc[...])
    weight = jnp.sum(coeff * coeff)
    lane = lax.broadcasted_iota(jnp.int32, (8, LANES), 1)
    row = lax.broadcasted_iota(jnp.int32, (8, LANES), 0)
    sums = jnp.where(lane == 0, projection, jnp.where(lane == 1, weight, 0.0))
    sums = jnp.where(row == 0, sums, 0.0)
    for there in range(8):
        for part in range(8):
            turn_ref[there, part * 32 : part * 32 + 32, :] = acc[
                there * 32 : there * 32 + 32, part * LANES : part * LANES + LANES
            ]
        turn_ref[there, 256:264, :] = sums
    for target in range(32):
        quarter, col = target // 8, target % 8
        for part in range(2):
            lanes = quarter * 256 + part * LANES
            for below in range(2):
                at = (2 * (col % 4) + below) * 32 + col // 4 * 16
                home_ref[target, part * 32 + below * 16 : part * 32 + below * 16 + 16, :] = acc[
                    at : at + 16, lanes : lanes + LANES
                ]


def multiply(place, blocks, halves):
    strings = blocks[0].shape[1]
    vmem = pl.BlockSpec(memory_space=pltpu.VMEM)
    return pl.pallas_call(
        product_kernel,
        in_specs=[pl.BlockSpec(memory_space=pltpu.SMEM)] + [vmem] * (len(blocks) + len(halves)),
        out_specs=[vmem, vmem],
        scratch_shapes=[
            pltpu.VMEM((256, CHUNK), jnp.bfloat16),
            pltpu.VMEM((256, 1024), jnp.float32),
            pltpu.VMEM((256, 1024), jnp.bfloat16),
        ],
        out_shape=[
            jax.ShapeDtypeStruct((8, 264, LANES), jnp.float32),
            jax.ShapeDtypeStruct((32, 64, LANES), jnp.float32),
        ],
        compiler_params=pltpu.CompilerParams(vmem_limit_bytes=30 * MIB),
        cost_estimate=pl.CostEstimate(
            flops=2 * 256 * 1024 * strings, bytes_accessed=24 * MIB, transcendentals=0
        ),
    )(place, *blocks, *halves)


def split_kernel(value_ref, out_ref, start):
    out_ref[...] = value_ref[start : start + out_ref.shape[0], :]


def take_rows(value, start):
    rows, cols = value.shape
    return pl.pallas_call(
        functools.partial(split_kernel, start=start),
        out_shape=jax.ShapeDtypeStruct((rows // 2, cols), value.dtype),
        compiler_params=pltpu.CompilerParams(vmem_limit_bytes=3 * MIB),
    )(value)


def pack_kernel(turn_ref, home_ref, out_ref):
    sums = jnp.sum(turn_ref[:, 256:264, :], axis=0)
    for target in range(32):
        row, col = target // 8, target % 8
        out_ref[target, 0:64, :] = home_ref[target, :, :]
        for part in range(8):
            source = ((col // 4) * 4 + part % 4) * 32 + row * 8
            out_ref[target, 64 + part * 8 : 72 + part * 8, :] = turn_ref[
                2 * (col % 4) + part // 4, source : source + 8, :
            ]
        out_ref[target, 128:136, :] = sums


def pack(turn, home):
    return pl.pallas_call(
        pack_kernel,
        out_shape=jax.ShapeDtypeStruct((32, 136, LANES), jnp.float32),
        compiler_params=pltpu.CompilerParams(vmem_limit_bytes=16 * MIB),
        cost_estimate=pl.CostEstimate(flops=0, bytes_accessed=5 * MIB, transcendentals=0),
    )(turn, home)


def finish_kernel(update_ref, totals_ref, own_ref, out_ref, stats_ref):
    totals = jnp.sum(totals_ref[...], axis=0, keepdims=True) * (1.0 / (NS * NS))
    lane = lax.broadcasted_iota(jnp.int32, (1, LANES), 1)
    spread = jnp.sum(jnp.where(lane == 0, totals, 0.0), axis=1, keepdims=True)
    out_ref[...] = update_ref[...] * lax.rsqrt(spread + 1e-06)
    stats_ref[...] = jnp.where(lane == 0, own_ref[0:1, :], jnp.sqrt(totals))


def finish(update, totals, own):
    return pl.pallas_call(
        finish_kernel,
        out_shape=[
            jax.ShapeDtypeStruct(update.shape, jnp.float32),
            jax.ShapeDtypeStruct((1, LANES), jnp.float32),
        ],
        compiler_params=pltpu.CompilerParams(vmem_limit_bytes=16 * MIB),
        cost_estimate=pl.CostEstimate(flops=update.size, bytes_accessed=2 * MIB, transcendentals=0),
    )(update, totals, own)


def update_kernel(tiles_ref, coeff_ref, diag_ref, update_ref, sums_ref, theta_ref):
    totals = jnp.sum(tiles_ref[:, 128:136, :], axis=0)
    lane = lax.broadcasted_iota(jnp.int32, (8, LANES), 1)
    projection = jnp.sum(jnp.where(lane == 0, totals, 0.0))
    weight = jnp.sum(jnp.where(lane == 1, totals, 0.0))
    theta = jnp.full((1, 1), projection) / jnp.full((1, 1), weight)
    squares = jnp.zeros((8, LANES), jnp.float32)
    spread = jnp.zeros((8, LANES), jnp.float32)
    for part in range(2):
        rows = slice(part * LANES, part * LANES + LANES)
        for index in range(8):
            cols = slice(index * LANES, index * LANES + LANES)
            quarter, group = index // 2, index % 2
            at = part * 32 + quarter * 8
            straight = tiles_ref[group * 16 : group * 16 + 16, at : at + 8, :]
            straight = straight.reshape(LANES, LANES).T
            turned = tiles_ref[part * 16 : part * 16 + 16, 64 + index * 8 : 72 + index * 8, :]
            turned = turned.reshape(LANES, LANES)
            coeff = coeff_ref[rows, cols].astype(jnp.float32)
            residual = straight + turned - theta * coeff
            update = residual / jnp.maximum(jnp.abs(diag_ref[rows, cols] - theta), 1.0)
            update_ref[rows, cols] = update
            squares += jnp.sum((residual * residual).reshape(16, 8, LANES), axis=0)
            spread += jnp.sum((update * update).reshape(16, 8, LANES), axis=0)
    theta_ref[...] = jnp.broadcast_to(theta, theta_ref.shape)
    values = jnp.where(lane == 0, jnp.sum(spread), jnp.where(lane == 1, jnp.sum(squares), 0.0))
    sums_ref[...] = jnp.broadcast_to(values[0:1, :], sums_ref.shape)


def make_update(tiles, coeff, diagonal):
    return pl.pallas_call(
        update_kernel,
        out_shape=[
            jax.ShapeDtypeStruct(coeff.shape, jnp.float32),
            jax.ShapeDtypeStruct((256, LANES), jnp.float32),
            jax.ShapeDtypeStruct((8, LANES), jnp.float32),
        ],
        compiler_params=pltpu.CompilerParams(vmem_limit_bytes=16 * MIB),
        cost_estimate=pl.CostEstimate(
            flops=10 * coeff.size, bytes_accessed=5 * MIB, transcendentals=0
        ),
    )(tiles, coeff, diagonal)


def swap(value):
    return lax.ppermute(value, "core", [(0, 1), (1, 0)])


def shift(value, step):
    count = lax.axis_size("z")
    return lax.ppermute(value, "z", [(i, (i + step) % count) for i in range(count)])


def shift_x(value, step):
    def index(x):
        return x % 2 * 2 + x // 2

    pairs = [(index(x), index((x + step) % 4)) for x in range(4)]
    return lax.ppermute(value, ("xlo", "xhi"), pairs)


def exchange(value, axes):
    return lax.all_to_all(value, axes, split_axis=0, concat_axis=0, tiled=True)


def body(ham, coeff, tile_mask, occupation, orbital_energy, coulomb):
    rows, strings = ham.shape
    cols = coeff.shape[1]
    core = lax.axis_index("core")
    xlo = lax.axis_index("xlo")
    z = lax.axis_index("z")
    row_index = (xlo * 8 + z) * 2 + core
    col_index = lax.axis_index("xhi") * 4 + lax.axis_index("y")

    place = jnp.stack([xlo, z, core]).astype(jnp.int32)
    ham, place = lax.optimization_barrier((ham, place))
    pair, pair_mask = swap(ham), swap(tile_mask)
    own_a, own_b = mask_half(ham, tile_mask, 0), mask_half(ham, tile_mask, 1)
    pair_a, pair_b = mask_half(pair, pair_mask, 0), mask_half(pair, pair_mask, 1)

    block = exchange(coeff.reshape(32, 8, cols), PLANE)
    block = block.reshape(4, 8, 8, cols).transpose(0, 2, 1, 3).reshape(32, strings)
    block, own_a, own_b, pair_a, pair_b = lax.optimization_barrier(
        (block, own_a, own_b, pair_a, pair_b)
    )
    far_a, far_b = shift_x(own_a, 1), shift_x(own_b, -1)
    p1, m1 = lax.optimization_barrier((shift(block, 1), shift(block, -1)))
    p2, m2 = lax.optimization_barrier((shift(p1, 1), shift(m1, -1)))
    p3, m3, far_a, far_b = lax.optimization_barrier((shift(p2, 1), shift(m2, -1), far_a, far_b))
    cross_a, cross_b = swap(far_a), swap(far_b)
    top, low = shift(take_rows(p3, 0), 1), shift(take_rows(m3, 16), -1)

    turn, home = multiply(
        place,
        (block, p1, p2, p3, m1, m2, m3, top, low),
        (own_a, own_b, pair_a, pair_b, far_a, far_b, cross_a, cross_b),
    )

    tiles = exchange(pack(exchange(turn, "z"), home), PLANE)

    occ_float = occupation.astype(jnp.float32)
    occ_alpha = lax.dynamic_slice_in_dim(occ_float, row_index * rows, rows, 1)
    occ_beta = lax.dynamic_slice_in_dim(occ_float, col_index * cols, cols, 1)
    energy_alpha = jnp.dot(orbital_energy, occ_alpha, precision=lax.Precision.HIGHEST)
    energy_beta = jnp.dot(orbital_energy, occ_beta, precision=lax.Precision.HIGHEST)
    coupling = jnp.dot(
        jnp.dot(occ_alpha.T, coulomb, precision=lax.Precision.HIGHEST),
        occ_beta,
        precision=lax.Precision.HIGHEST,
    )
    diagonal = energy_alpha[:, None] + energy_beta[None, :] + coupling

    update, sums, theta = make_update(tiles, coeff, diagonal)
    correction, stats = finish(update, exchange(sums, AXES), theta)
    return (correction, stats[0, :2])


def solution(mesh):
    fine = Mesh(mesh.devices.reshape(SIZES), AXES)
    in_specs = (P(ROW, None), P(ROW, COL), P(ROW, None), P(), P(), P())
    out_specs = (P(ROW, COL), P())
    return jax.shard_map(body, mesh=fine, in_specs=in_specs, out_specs=out_specs, check_vma=False)
```

```python
import functools

import jax
import jax.numpy as jnp
from jax import lax
from jax.experimental import pallas as pl
from jax.experimental.pallas import tpu as pltpu
from jax.sharding import Mesh, PartitionSpec as P

NS = 8192
AXES = ("xlo", "z", "core", "xhi", "y")
SIZES = (2, 8, 2, 2, 4)
ROW = ("xlo", "z", "core")
COL = ("xhi", "y")
PLANE = ("xlo", "core", "xhi", "y")
LANES = 128
CHUNK = 1024
MIB = 1024 * 1024


def mask_kernel(ham_ref, mask_ref, out_ref):
    rows, cols = ham_ref.shape
    mask_rows, mask_cols = mask_ref.shape
    tile = size = rows // mask_rows
    spread = (
        lax.broadcasted_iota(jnp.int32, (mask_cols, cols), 1) // size + pl.program_id(0) * (cols // size)
        == lax.broadcasted_iota(jnp.int32, (mask_cols, cols), 0)
    ).astype(jnp.bfloat16)
    mask = mask_ref[...].astype(jnp.float32).astype(jnp.bfloat16)
    wide = jnp.dot(mask, spread, preferred_element_type=jnp.float32)
    for index in range(mask_rows):
        at = index * tile
        values = ham_ref[at : at + tile, :].astype(jnp.float32) * wide[index : index + 1, :]
        out_ref[at : at + tile, :] = values.astype(jnp.bfloat16)


def mask_half(ham, tile_mask, half):
    rows, cols = ham.shape
    mask_rows, mask_cols = tile_mask.shape
    return pl.pallas_call(
        mask_kernel,
        grid=(4,),
        in_specs=[
            pl.BlockSpec((rows, cols // 8), lambda j: (0, half * 4 + j)),
            pl.BlockSpec((mask_rows, mask_cols // 2), lambda j: (0, half)),
        ],
        out_specs=pl.BlockSpec((rows, cols // 8), lambda j: (0, j)),
        out_shape=jax.ShapeDtypeStruct((rows, cols // 2), jnp.bfloat16),
        compiler_params=pltpu.CompilerParams(vmem_limit_bytes=8 * MIB),
        cost_estimate=pl.CostEstimate(
            flops=rows * cols, bytes_accessed=2 * rows * cols, transcendentals=0
        ),
    )(ham, tile_mask)


def product_kernel(
    place_ref, c0, p1, p2, p3, m1, m2, m3, top, low,
    own_a, own_b, pair_a, pair_b, far_a, far_b, cross_a, cross_b,
    turn_ref, home_ref, lhs, acc, local,
):
    xlo, z, core = place_ref[0], place_ref[1], place_ref[2]
    strings = c0.shape[1]
    blocks = ((0, c0), (-1, p1), (-2, p2), (-3, p3), (1, m1), (2, m2), (3, m3))
    acc[...] = jnp.zeros_like(acc)

    def gather(at, width, out):
        for offset, ref in blocks:
            row = pl.multiple_of(lax.rem(z + offset + 8, 8) * 32, 32)
            out[pl.ds(row, 32), :] = ref[:, pl.ds(at, width)]
        row = pl.multiple_of(lax.rem(z + 4, 8) * 32, 32)
        out[pl.ds(row, 16), :] = top[:, pl.ds(at, width)]
        out[pl.ds(pl.multiple_of(row + 16, 16), 16), :] = low[:, pl.ds(at, width)]

    for start, panels in (
        (0, (own_a, pair_a, far_a, cross_a)),
        (strings // 2, (own_b, pair_b, far_b, cross_b)),
    ):

        def step(index, carry, start=start, panels=panels):
            at = pl.multiple_of(index * CHUNK, CHUNK)
            gather(pl.multiple_of(start + at, CHUNK), CHUNK, lhs)
            for number, ref in enumerate(panels):
                side = xlo if number < 2 else 1 - xlo
                other = core if number % 2 == 0 else 1 - core
                columns = pl.ds(pl.multiple_of((side * 2 + other) * 256, 256), 256)
                acc[:, columns] += lax.dot_general(
                    lhs[...],
                    ref[:, pl.ds(at, CHUNK)],
                    (((1,), (1,)), ((), ())),
                    preferred_element_type=jnp.float32,
                )
            return carry

        lax.fori_loop(0, strings // 2 // CHUNK, step, 0)

    for side in range(2):
        at = pl.multiple_of(side * (strings // 2) + z * 512, 512)
        gather(at, 512, local.at[:, side * 512 : side * 512 + 512])

    coeff = local[...].astype(jnp.float32)
    projection = jnp.sum(2.0 * coeff * acc[...])
    weight = jnp.sum(coeff * coeff)
    lane = lax.broadcasted_iota(jnp.int32, (8, LANES), 1)
    row = lax.broadcasted_iota(jnp.int32, (8, LANES), 0)
    sums = jnp.where(lane == 0, projection, jnp.where(lane == 1, weight, 0.0))
    sums = jnp.where(row == 0, sums, 0.0)
    for there in range(8):
        for part in range(8):
            turn_ref[there, part * 32 : part * 32 + 32, :] = acc[
                there * 32 : there * 32 + 32, part * LANES : part * LANES + LANES
            ]
        turn_ref[there, 256:264, :] = sums
    for target in range(32):
        quarter, col = target // 8, target % 8
        for part in range(2):
            lanes = quarter * 256 + part * LANES
            for below in range(2):
                at = (2 * (col % 4) + below) * 32 + col // 4 * 16
                home_ref[target, part * 32 + below * 16 : part * 32 + below * 16 + 16, :] = acc[
                    at : at + 16, lanes : lanes + LANES
                ]


def multiply(place, blocks, halves):
    strings = blocks[0].shape[1]
    vmem = pl.BlockSpec(memory_space=pltpu.VMEM)
    return pl.pallas_call(
        product_kernel,
        in_specs=[pl.BlockSpec(memory_space=pltpu.SMEM)] + [vmem] * (len(blocks) + len(halves)),
        out_specs=[vmem, vmem],
        scratch_shapes=[
            pltpu.VMEM((256, CHUNK), jnp.bfloat16),
            pltpu.VMEM((256, 1024), jnp.float32),
            pltpu.VMEM((256, 1024), jnp.bfloat16),
        ],
        out_shape=[
            jax.ShapeDtypeStruct((8, 264, LANES), jnp.float32),
            jax.ShapeDtypeStruct((32, 64, LANES), jnp.float32),
        ],
        compiler_params=pltpu.CompilerParams(vmem_limit_bytes=30 * MIB),
        cost_estimate=pl.CostEstimate(
            flops=2 * 256 * 1024 * strings, bytes_accessed=24 * MIB, transcendentals=0
        ),
    )(place, *blocks, *halves)


def split_kernel(value_ref, out_ref, start):
    out_ref[...] = value_ref[start : start + out_ref.shape[0], :]


def take_rows(value, start):
    rows, cols = value.shape
    return pl.pallas_call(
        functools.partial(split_kernel, start=start),
        out_shape=jax.ShapeDtypeStruct((rows // 2, cols), value.dtype),
        compiler_params=pltpu.CompilerParams(vmem_limit_bytes=3 * MIB),
    )(value)


def pack_kernel(turn_ref, home_ref, out_ref):
    sums = jnp.sum(turn_ref[:, 256:264, :], axis=0)
    for target in range(32):
        row, col = target // 8, target % 8
        out_ref[target, 0:64, :] = home_ref[target, :, :]
        for part in range(8):
            source = ((col // 4) * 4 + part % 4) * 32 + row * 8
            out_ref[target, 64 + part * 8 : 72 + part * 8, :] = turn_ref[
                2 * (col % 4) + part // 4, source : source + 8, :
            ]
        out_ref[target, 128:136, :] = sums


def pack(turn, home):
    return pl.pallas_call(
        pack_kernel,
        out_shape=jax.ShapeDtypeStruct((32, 136, LANES), jnp.float32),
        compiler_params=pltpu.CompilerParams(vmem_limit_bytes=16 * MIB),
        cost_estimate=pl.CostEstimate(flops=0, bytes_accessed=5 * MIB, transcendentals=0),
    )(turn, home)


def finish_kernel(update_ref, totals_ref, own_ref, out_ref, stats_ref):
    totals = jnp.sum(totals_ref[...], axis=0, keepdims=True) * (1.0 / (NS * NS))
    lane = lax.broadcasted_iota(jnp.int32, (1, LANES), 1)
    spread = jnp.sum(jnp.where(lane == 0, totals, 0.0), axis=1, keepdims=True)
    out_ref[...] = update_ref[...] * lax.rsqrt(spread + 1e-06)
    stats_ref[...] = jnp.where(lane == 0, own_ref[0:1, :], jnp.sqrt(totals))


def finish(update, totals, own):
    return pl.pallas_call(
        finish_kernel,
        out_shape=[
            jax.ShapeDtypeStruct(update.shape, jnp.float32),
            jax.ShapeDtypeStruct((1, LANES), jnp.float32),
        ],
        compiler_params=pltpu.CompilerParams(vmem_limit_bytes=16 * MIB),
        cost_estimate=pl.CostEstimate(flops=update.size, bytes_accessed=2 * MIB, transcendentals=0),
    )(update, totals, own)


def update_kernel(tiles_ref, coeff_ref, diag_ref, update_ref, sums_ref, theta_ref):
    totals = jnp.sum(tiles_ref[:, 128:136, :], axis=0)
    lane = lax.broadcasted_iota(jnp.int32, (8, LANES), 1)
    projection = jnp.sum(jnp.where(lane == 0, totals, 0.0))
    weight = jnp.sum(jnp.where(lane == 1, totals, 0.0))
    theta = jnp.full((1, 1), projection) / jnp.full((1, 1), weight)
    squares = jnp.zeros((8, LANES), jnp.float32)
    spread = jnp.zeros((8, LANES), jnp.float32)
    for part in range(2):
        rows = slice(part * LANES, part * LANES + LANES)
        for index in range(8):
            cols = slice(index * LANES, index * LANES + LANES)
            quarter, group = index // 2, index % 2
            at = part * 32 + quarter * 8
            straight = tiles_ref[group * 16 : group * 16 + 16, at : at + 8, :]
            straight = straight.reshape(LANES, LANES).T
            turned = tiles_ref[part * 16 : part * 16 + 16, 64 + index * 8 : 72 + index * 8, :]
            turned = turned.reshape(LANES, LANES)
            coeff = coeff_ref[rows, cols].astype(jnp.float32)
            residual = straight + turned - theta * coeff
            update = residual / jnp.maximum(jnp.abs(diag_ref[rows, cols] - theta), 1.0)
            update_ref[rows, cols] = update
            squares += jnp.sum((residual * residual).reshape(16, 8, LANES), axis=0)
            spread += jnp.sum((update * update).reshape(16, 8, LANES), axis=0)
    theta_ref[...] = jnp.broadcast_to(theta, theta_ref.shape)
    values = jnp.where(lane == 0, jnp.sum(spread), jnp.where(lane == 1, jnp.sum(squares), 0.0))
    sums_ref[...] = jnp.broadcast_to(values[0:1, :], sums_ref.shape)


def make_update(tiles, coeff, diagonal):
    return pl.pallas_call(
        update_kernel,
        out_shape=[
            jax.ShapeDtypeStruct(coeff.shape, jnp.float32),
            jax.ShapeDtypeStruct((256, LANES), jnp.float32),
            jax.ShapeDtypeStruct((8, LANES), jnp.float32),
        ],
        compiler_params=pltpu.CompilerParams(vmem_limit_bytes=16 * MIB),
        cost_estimate=pl.CostEstimate(
            flops=10 * coeff.size, bytes_accessed=5 * MIB, transcendentals=0
        ),
    )(tiles, coeff, diagonal)


def swap(value):
    return lax.ppermute(value, "core", [(0, 1), (1, 0)])


def shift(value, step):
    count = lax.axis_size("z")
    return lax.ppermute(value, "z", [(i, (i + step) % count) for i in range(count)])


def shift_x(value, step):
    def index(x):
        return x % 2 * 2 + x // 2

    pairs = [(index(x), index((x + step) % 4)) for x in range(4)]
    return lax.ppermute(value, ("xlo", "xhi"), pairs)


def exchange(value, axes):
    return lax.all_to_all(value, axes, split_axis=0, concat_axis=0, tiled=True)


def body(ham, coeff, tile_mask, occupation, orbital_energy, coulomb):
    rows, strings = ham.shape
    cols = coeff.shape[1]
    core = lax.axis_index("core")
    xlo = lax.axis_index("xlo")
    z = lax.axis_index("z")
    row_index = (xlo * 8 + z) * 2 + core
    col_index = lax.axis_index("xhi") * 4 + lax.axis_index("y")

    place = jnp.stack([xlo, z, core]).astype(jnp.int32)
    ham, place = lax.optimization_barrier((ham, place))
    pair, pair_mask = swap(ham), swap(tile_mask)
    own_a, own_b = mask_half(ham, tile_mask, 0), mask_half(ham, tile_mask, 1)

    block = exchange(coeff.reshape(32, 8, cols), PLANE)
    block = block.reshape(4, 8, 8, cols).transpose(0, 2, 1, 3).reshape(32, strings)
    block, own_a, own_b, pair, pair_mask = lax.optimization_barrier(
        (block, own_a, own_b, pair, pair_mask)
    )
    far_a, far_b = shift_x(own_a, 1), shift_x(own_b, -1)
    p1, m1, pair, pair_mask = lax.optimization_barrier(
        (shift(block, 1), shift(block, -1), pair, pair_mask)
    )
    pair_a, pair_b = mask_half(pair, pair_mask, 0), mask_half(pair, pair_mask, 1)
    p2, m2, pair_a, pair_b = lax.optimization_barrier(
        (shift(p1, 1), shift(m1, -1), pair_a, pair_b)
    )
    p3, m3 = shift(p2, 1), shift(m2, -1)
    top, low = take_rows(p3, 0), take_rows(m3, 16)
    _, _, far_a, far_b = lax.optimization_barrier((top, low, far_a, far_b))
    top, low = shift(top, 1), shift(low, -1)
    cross_a, cross_b = swap(far_a), swap(far_b)

    turn, home = multiply(
        place,
        (block, p1, p2, p3, m1, m2, m3, top, low),
        (own_a, own_b, pair_a, pair_b, far_a, far_b, cross_a, cross_b),
    )

    tiles = exchange(pack(exchange(turn, "z"), home), PLANE)

    occ_float = occupation.astype(jnp.float32)
    occ_alpha = lax.dynamic_slice_in_dim(occ_float, row_index * rows, rows, 1)
    occ_beta = lax.dynamic_slice_in_dim(occ_float, col_index * cols, cols, 1)
    energy_alpha = jnp.dot(orbital_energy, occ_alpha, precision=lax.Precision.HIGHEST)
    energy_beta = jnp.dot(orbital_energy, occ_beta, precision=lax.Precision.HIGHEST)
    coupling = jnp.dot(
        jnp.dot(occ_alpha.T, coulomb, precision=lax.Precision.HIGHEST),
        occ_beta,
        precision=lax.Precision.HIGHEST,
    )
    diagonal = energy_alpha[:, None] + energy_beta[None, :] + coupling

    update, sums, theta = make_update(tiles, coeff, diagonal)
    correction, stats = finish(update, exchange(sums, AXES), theta)
    return (correction, stats[0, :2])


def solution(mesh):
    fine = Mesh(mesh.devices.reshape(SIZES), AXES)
    in_specs = (P(ROW, None), P(ROW, COL), P(ROW, None), P(), P(), P())
    out_specs = (P(ROW, COL), P())
    return jax.shard_map(body, mesh=fine, in_specs=in_specs, out_specs=out_specs, check_vma=False)
```

```python
import functools

import jax
import jax.numpy as jnp
from jax import lax
from jax.experimental import pallas as pl
from jax.experimental.pallas import tpu as pltpu
from jax.sharding import Mesh, PartitionSpec as P

NS = 8192
AXES = ("xlo", "z", "core", "xhi", "y")
SIZES = (2, 8, 2, 2, 4)
ROW = ("xlo", "z", "core")
COL = ("xhi", "y")
PLANE = ("xlo", "core", "xhi", "y")
LANES = 128
CHUNK = 1024
MIB = 1024 * 1024


def mask_kernel(ham_ref, mask_ref, out_ref):
    rows, cols = ham_ref.shape
    mask_rows, mask_cols = mask_ref.shape
    tile = size = rows // mask_rows
    spread = (
        lax.broadcasted_iota(jnp.int32, (mask_cols, cols), 1) // size + pl.program_id(0) * (cols // size)
        == lax.broadcasted_iota(jnp.int32, (mask_cols, cols), 0)
    ).astype(jnp.bfloat16)
    mask = mask_ref[...].astype(jnp.float32).astype(jnp.bfloat16)
    wide = jnp.dot(mask, spread, preferred_element_type=jnp.float32)
    for index in range(mask_rows):
        at = index * tile
        values = ham_ref[at : at + tile, :].astype(jnp.float32) * wide[index : index + 1, :]
        out_ref[at : at + tile, :] = values.astype(jnp.bfloat16)


def mask_rows_of(ham, tile_mask):
    rows, cols = ham.shape
    mask_rows, mask_cols = tile_mask.shape
    return pl.pallas_call(
        mask_kernel,
        grid=(cols // CHUNK,),
        in_specs=[
            pl.BlockSpec((rows, CHUNK), lambda j: (0, j)),
            pl.BlockSpec((mask_rows, mask_cols), lambda j: (0, 0)),
        ],
        out_specs=pl.BlockSpec((rows, CHUNK), lambda j: (0, j)),
        out_shape=jax.ShapeDtypeStruct((rows, cols), jnp.bfloat16),
        compiler_params=pltpu.CompilerParams(vmem_limit_bytes=8 * MIB),
        cost_estimate=pl.CostEstimate(
            flops=2 * rows * cols, bytes_accessed=4 * rows * cols, transcendentals=0
        ),
    )(ham, tile_mask)


def part_kernel(place_ref, ham_ref, mask_ref, *out_refs):
    rows = ham_ref.shape[0]
    mask_rows, mask_cols = mask_ref.shape
    tile = rows // mask_rows
    mask = mask_ref[...].astype(jnp.float32).astype(jnp.bfloat16)
    parts = [(place_ref[3] * 2, out_refs[0], 0), (place_ref[3] * 2 + 1, out_refs[1], 0)]
    parts += [(4 + index, out_refs[2 + index // 2], index % 2 * CHUNK) for index in range(4)]
    for chunk, out_ref, start in parts:
        column = lax.broadcasted_iota(jnp.int32, (mask_cols, CHUNK), 1)
        spread = (
            column // tile + chunk * (CHUNK // tile)
            == lax.broadcasted_iota(jnp.int32, (mask_cols, CHUNK), 0)
        ).astype(jnp.bfloat16)
        wide = jnp.dot(mask, spread, preferred_element_type=jnp.float32)
        columns = pl.ds(chunk * CHUNK, CHUNK)
        if not isinstance(chunk, int):
            columns = pl.ds(pl.multiple_of(chunk * CHUNK, CHUNK), CHUNK)
        for row in range(mask_rows):
            at = row * tile
            values = ham_ref[at : at + tile, columns].astype(jnp.float32) * wide[row : row + 1, :]
            out_ref[at : at + tile, start : start + CHUNK] = values.astype(jnp.bfloat16)


def mask_part(place, ham, tile_mask):
    rows, cols = ham.shape
    vmem = pl.BlockSpec(memory_space=pltpu.VMEM)
    return pl.pallas_call(
        part_kernel,
        in_specs=[pl.BlockSpec(memory_space=pltpu.SMEM), vmem, vmem],
        out_specs=[vmem] * 4,
        out_shape=[
            jax.ShapeDtypeStruct((rows, width), jnp.bfloat16)
            for width in (CHUNK, CHUNK, 2 * CHUNK, 2 * CHUNK)
        ],
        compiler_params=pltpu.CompilerParams(vmem_limit_bytes=12 * MIB),
        cost_estimate=pl.CostEstimate(
            flops=rows * cols, bytes_accessed=2 * rows * cols, transcendentals=0
        ),
    )(place, ham, tile_mask)


def product_kernel(
    place_ref, c0, p1, p2, p3, m1, m2, m3, top, low,
    own, pair, f0, f2, g0, g2, fa, fb, x0, x2, w0, w2, xa, xb,
    turn_ref, home_ref, lhs, acc, local,
):
    xlo, z, core = place_ref[0], place_ref[1], place_ref[2]
    strings = c0.shape[1]
    blocks = ((0, c0), (-1, p1), (-2, p2), (-3, p3), (1, m1), (2, m2), (3, m3))
    acc[...] = jnp.zeros_like(acc)

    def gather(at, width, out):
        for offset, ref in blocks:
            row = pl.multiple_of(lax.rem(z + offset + 8, 8) * 32, 32)
            out[pl.ds(row, 32), :] = ref[:, pl.ds(at, width)]
        row = pl.multiple_of(lax.rem(z + 4, 8) * 32, 32)
        out[pl.ds(row, 16), :] = top[:, pl.ds(at, width)]
        out[pl.ds(pl.multiple_of(row + 16, 16), 16), :] = low[:, pl.ds(at, width)]

    parity = place_ref[3]
    steps = [
        (2 * parity, f0, x0, 0), (2 * parity + 1, f2, x2, 0),
        (2 - 2 * parity, g0, w0, 0), (3 - 2 * parity, g2, w2, 0),
        (4, fa, xa, 0), (5, fa, xa, CHUNK), (6, fb, xb, 0), (7, fb, xb, CHUNK),
    ]
    for chunk, far, cross, start in steps:
        at = pl.multiple_of(chunk * CHUNK, CHUNK)
        gather(at, CHUNK, lhs)
        part = slice(start, start + CHUNK)
        here = pl.ds(at, CHUNK)
        for number, panel in enumerate((own[:, here], pair[:, here], far[:, part], cross[:, part])):
            side = xlo if number < 2 else 1 - xlo
            other = core if number % 2 == 0 else 1 - core
            columns = pl.ds(pl.multiple_of((side * 2 + other) * 256, 256), 256)
            acc[:, columns] += lax.dot_general(
                lhs[...], panel, (((1,), (1,)), ((), ())), preferred_element_type=jnp.float32
            )

    for side in range(2):
        at = pl.multiple_of(side * (strings // 2) + z * 512, 512)
        gather(at, 512, local.at[:, side * 512 : side * 512 + 512])

    coeff = local[...].astype(jnp.float32)
    projection = jnp.sum(2.0 * coeff * acc[...])
    weight = jnp.sum(coeff * coeff)
    lane = lax.broadcasted_iota(jnp.int32, (8, LANES), 1)
    row = lax.broadcasted_iota(jnp.int32, (8, LANES), 0)
    sums = jnp.where(lane == 0, projection, jnp.where(lane == 1, weight, 0.0))
    sums = jnp.where(row == 0, sums, 0.0)
    for there in range(8):
        for part in range(8):
            turn_ref[there, part * 32 : part * 32 + 32, :] = acc[
                there * 32 : there * 32 + 32, part * LANES : part * LANES + LANES
            ]
        turn_ref[there, 256:264, :] = sums
    for target in range(32):
        quarter, col = target // 8, target % 8
        for part in range(2):
            lanes = quarter * 256 + part * LANES
            for below in range(2):
                at = (2 * (col % 4) + below) * 32 + col // 4 * 16
                home_ref[target, part * 32 + below * 16 : part * 32 + below * 16 + 16, :] = acc[
                    at : at + 16, lanes : lanes + LANES
                ]


def multiply(place, blocks, halves):
    strings = blocks[0].shape[1]
    vmem = pl.BlockSpec(memory_space=pltpu.VMEM)
    return pl.pallas_call(
        product_kernel,
        in_specs=[pl.BlockSpec(memory_space=pltpu.SMEM)] + [vmem] * (len(blocks) + len(halves)),
        out_specs=[vmem, vmem],
        scratch_shapes=[
            pltpu.VMEM((256, CHUNK), jnp.bfloat16),
            pltpu.VMEM((256, 1024), jnp.float32),
            pltpu.VMEM((256, 1024), jnp.bfloat16),
        ],
        out_shape=[
            jax.ShapeDtypeStruct((8, 264, LANES), jnp.float32),
            jax.ShapeDtypeStruct((32, 64, LANES), jnp.float32),
        ],
        compiler_params=pltpu.CompilerParams(vmem_limit_bytes=30 * MIB),
        cost_estimate=pl.CostEstimate(
            flops=2 * 256 * 1024 * strings, bytes_accessed=24 * MIB, transcendentals=0
        ),
    )(place, *blocks, *halves)


def split_kernel(value_ref, out_ref, start):
    out_ref[...] = value_ref[start : start + out_ref.shape[0], :]


def take_rows(value, start):
    rows, cols = value.shape
    return pl.pallas_call(
        functools.partial(split_kernel, start=start),
        out_shape=jax.ShapeDtypeStruct((rows // 2, cols), value.dtype),
        compiler_params=pltpu.CompilerParams(vmem_limit_bytes=3 * MIB),
    )(value)


def pack_kernel(turn_ref, home_ref, out_ref):
    sums = jnp.sum(turn_ref[:, 256:264, :], axis=0)
    for target in range(32):
        row, col = target // 8, target % 8
        out_ref[target, 0:64, :] = home_ref[target, :, :]
        for part in range(8):
            source = ((col // 4) * 4 + part % 4) * 32 + row * 8
            out_ref[target, 64 + part * 8 : 72 + part * 8, :] = turn_ref[
                2 * (col % 4) + part // 4, source : source + 8, :
            ]
        out_ref[target, 128:136, :] = sums


def pack(turn, home):
    return pl.pallas_call(
        pack_kernel,
        out_shape=jax.ShapeDtypeStruct((32, 136, LANES), jnp.float32),
        compiler_params=pltpu.CompilerParams(vmem_limit_bytes=16 * MIB),
        cost_estimate=pl.CostEstimate(flops=0, bytes_accessed=5 * MIB, transcendentals=0),
    )(turn, home)


def finish_kernel(update_ref, totals_ref, own_ref, out_ref, stats_ref):
    totals = jnp.sum(totals_ref[...], axis=0, keepdims=True) * (1.0 / (NS * NS))
    lane = lax.broadcasted_iota(jnp.int32, (1, LANES), 1)
    spread = jnp.sum(jnp.where(lane == 0, totals, 0.0), axis=1, keepdims=True)
    out_ref[...] = update_ref[...] * lax.rsqrt(spread + 1e-06)
    stats_ref[...] = jnp.where(lane == 0, own_ref[0:1, :], jnp.sqrt(totals))


def finish(update, totals, own):
    return pl.pallas_call(
        finish_kernel,
        out_shape=[
            jax.ShapeDtypeStruct(update.shape, jnp.float32),
            jax.ShapeDtypeStruct((1, LANES), jnp.float32),
        ],
        compiler_params=pltpu.CompilerParams(vmem_limit_bytes=16 * MIB),
        cost_estimate=pl.CostEstimate(flops=update.size, bytes_accessed=2 * MIB, transcendentals=0),
    )(update, totals, own)


def update_kernel(tiles_ref, coeff_ref, diag_ref, update_ref, sums_ref, theta_ref):
    totals = jnp.sum(tiles_ref[:, 128:136, :], axis=0)
    lane = lax.broadcasted_iota(jnp.int32, (8, LANES), 1)
    projection = jnp.sum(jnp.where(lane == 0, totals, 0.0))
    weight = jnp.sum(jnp.where(lane == 1, totals, 0.0))
    theta = jnp.full((1, 1), projection) / jnp.full((1, 1), weight)
    squares = jnp.zeros((8, LANES), jnp.float32)
    spread = jnp.zeros((8, LANES), jnp.float32)
    for part in range(2):
        rows = slice(part * LANES, part * LANES + LANES)
        for index in range(8):
            cols = slice(index * LANES, index * LANES + LANES)
            quarter, group = index // 2, index % 2
            at = part * 32 + quarter * 8
            straight = tiles_ref[group * 16 : group * 16 + 16, at : at + 8, :]
            straight = straight.reshape(LANES, LANES).T
            turned = tiles_ref[part * 16 : part * 16 + 16, 64 + index * 8 : 72 + index * 8, :]
            turned = turned.reshape(LANES, LANES)
            coeff = coeff_ref[rows, cols].astype(jnp.float32)
            residual = straight + turned - theta * coeff
            update = residual / jnp.maximum(jnp.abs(diag_ref[rows, cols] - theta), 1.0)
            update_ref[rows, cols] = update
            squares += jnp.sum((residual * residual).reshape(16, 8, LANES), axis=0)
            spread += jnp.sum((update * update).reshape(16, 8, LANES), axis=0)
    theta_ref[...] = jnp.broadcast_to(theta, theta_ref.shape)
    values = jnp.where(lane == 0, jnp.sum(spread), jnp.where(lane == 1, jnp.sum(squares), 0.0))
    sums_ref[...] = jnp.broadcast_to(values[0:1, :], sums_ref.shape)


def make_update(tiles, coeff, diagonal):
    return pl.pallas_call(
        update_kernel,
        out_shape=[
            jax.ShapeDtypeStruct(coeff.shape, jnp.float32),
            jax.ShapeDtypeStruct((256, LANES), jnp.float32),
            jax.ShapeDtypeStruct((8, LANES), jnp.float32),
        ],
        compiler_params=pltpu.CompilerParams(vmem_limit_bytes=16 * MIB),
        cost_estimate=pl.CostEstimate(
            flops=10 * coeff.size, bytes_accessed=5 * MIB, transcendentals=0
        ),
    )(tiles, coeff, diagonal)


def swap(value):
    return lax.ppermute(value, "core", [(0, 1), (1, 0)])


def shift(value, step):
    count = lax.axis_size("z")
    return lax.ppermute(value, "z", [(i, (i + step) % count) for i in range(count)])


def shift_x(value, step):
    def index(x):
        return x % 2 * 2 + x // 2

    pairs = [(index(x), index((x + step) % 4)) for x in range(4)]
    return lax.ppermute(value, ("xlo", "xhi"), pairs)


def shift_y(value, step):
    count = lax.axis_size("y")
    return lax.ppermute(value, "y", [(i, (i + step) % count) for i in range(count)])


def exchange(value, axes):
    return lax.all_to_all(value, axes, split_axis=0, concat_axis=0, tiled=True)


def body(ham, coeff, tile_mask, occupation, orbital_energy, coulomb):
    rows, strings = ham.shape
    cols = coeff.shape[1]
    core = lax.axis_index("core")
    xlo = lax.axis_index("xlo")
    z = lax.axis_index("z")
    row_index = (xlo * 8 + z) * 2 + core
    col_index = lax.axis_index("xhi") * 4 + lax.axis_index("y")

    parity = lax.rem(lax.axis_index("y"), 2)
    place = jnp.stack([xlo, z, core, parity]).astype(jnp.int32)
    ham, place = lax.optimization_barrier((ham, place))
    pair, pair_mask = swap(ham), swap(tile_mask)
    s0, s2, sa, sb = mask_part(place, ham, tile_mask)

    block = exchange(coeff.reshape(32, 8, cols), PLANE)
    block = block.reshape(4, 8, 8, cols).transpose(0, 2, 1, 3).reshape(32, strings)
    block, s0, s2, sa, sb, pair, pair_mask = lax.optimization_barrier(
        (block, s0, s2, sa, sb, pair, pair_mask)
    )
    p1, m1, f0, f2, sa, sb, ham, pair, pair_mask = lax.optimization_barrier(
        (
            shift(block, 1), shift(block, -1), shift_x(s0, 1), shift_x(s2, -1),
            sa, sb, ham, pair, pair_mask,
        )
    )
    fa, fb = shift_x(sa, 1), shift_x(sb, -1)
    own, pair = mask_rows_of(ham, tile_mask), mask_rows_of(pair, pair_mask)
    p2, m2, g0, f2, own, pair = lax.optimization_barrier(
        (shift(p1, 1), shift(m1, -1), shift_y(f0, 1), f2, own, pair)
    )
    p3, m3, g2, fa, fb, f0, f2, g0 = lax.optimization_barrier(
        (shift(p2, 1), shift(m2, -1), shift_y(f2, -1), fa, fb, f0, f2, g0)
    )
    top, low = shift(take_rows(p3, 0), 1), shift(take_rows(m3, 16), -1)
    x0, x2, w0, w2, xa, xb = (swap(value) for value in (f0, f2, g0, g2, fa, fb))

    turn, home = multiply(
        place,
        (block, p1, p2, p3, m1, m2, m3, top, low),
        (own, pair, f0, f2, g0, g2, fa, fb, x0, x2, w0, w2, xa, xb),
    )

    tiles = exchange(pack(exchange(turn, "z"), home), PLANE)

    occ_float = occupation.astype(jnp.float32)
    occ_alpha = lax.dynamic_slice_in_dim(occ_float, row_index * rows, rows, 1)
    occ_beta = lax.dynamic_slice_in_dim(occ_float, col_index * cols, cols, 1)
    energy_alpha = jnp.dot(orbital_energy, occ_alpha, precision=lax.Precision.HIGHEST)
    energy_beta = jnp.dot(orbital_energy, occ_beta, precision=lax.Precision.HIGHEST)
    coupling = jnp.dot(
        jnp.dot(occ_alpha.T, coulomb, precision=lax.Precision.HIGHEST),
        occ_beta,
        precision=lax.Precision.HIGHEST,
    )
    diagonal = energy_alpha[:, None] + energy_beta[None, :] + coupling

    update, sums, theta = make_update(tiles, coeff, diagonal)
    correction, stats = finish(update, exchange(sums, AXES), theta)
    return (correction, stats[0, :2])


def solution(mesh):
    fine = Mesh(mesh.devices.reshape(SIZES), AXES)
    in_specs = (P(ROW, None), P(ROW, COL), P(ROW, None), P(), P(), P())
    out_specs = (P(ROW, COL), P())
    return jax.shard_map(body, mesh=fine, in_specs=in_specs, out_specs=out_specs, check_vma=False)
```

```python
import functools

import jax
import jax.numpy as jnp
from jax import lax
from jax.experimental import pallas as pl
from jax.experimental.pallas import tpu as pltpu
from jax.sharding import Mesh, PartitionSpec as P

NS = 8192
AXES = ("xlo", "z", "core", "xhi", "y")
SIZES = (2, 8, 2, 2, 4)
ROW = ("xlo", "z", "core")
COL = ("xhi", "y")
PLANE = ("xlo", "core", "xhi", "y")
LANES = 128
CHUNK = 1024
MIB = 1024 * 1024


def mask_kernel(ham_ref, mask_ref, out_ref):
    rows, cols = ham_ref.shape
    mask_rows, mask_cols = mask_ref.shape
    tile = size = rows // mask_rows
    spread = (
        lax.broadcasted_iota(jnp.int32, (mask_cols, cols), 1) // size + pl.program_id(0) * (cols // size)
        == lax.broadcasted_iota(jnp.int32, (mask_cols, cols), 0)
    ).astype(jnp.bfloat16)
    mask = mask_ref[...].astype(jnp.float32).astype(jnp.bfloat16)
    wide = jnp.dot(mask, spread, preferred_element_type=jnp.float32)
    for index in range(mask_rows):
        at = index * tile
        values = ham_ref[at : at + tile, :].astype(jnp.float32) * wide[index : index + 1, :]
        out_ref[at : at + tile, :] = values.astype(jnp.bfloat16)


def mask_half(ham, tile_mask, half):
    rows, cols = ham.shape
    mask_rows, mask_cols = tile_mask.shape
    return pl.pallas_call(
        mask_kernel,
        grid=(4,),
        in_specs=[
            pl.BlockSpec((rows, cols // 8), lambda j: (0, half * 4 + j)),
            pl.BlockSpec((mask_rows, mask_cols // 2), lambda j: (0, half)),
        ],
        out_specs=pl.BlockSpec((rows, cols // 8), lambda j: (0, j)),
        out_shape=jax.ShapeDtypeStruct((rows, cols // 2), jnp.bfloat16),
        compiler_params=pltpu.CompilerParams(vmem_limit_bytes=8 * MIB),
        cost_estimate=pl.CostEstimate(
            flops=rows * cols, bytes_accessed=2 * rows * cols, transcendentals=0
        ),
    )(ham, tile_mask)


def collect(z, blocks, at, width, out_ref):
    c0, p1, p2, p3, m1, m2, m3, top, low = blocks
    for offset, ref in ((0, c0), (-1, p1), (-2, p2), (-3, p3), (1, m1), (2, m2), (3, m3)):
        row = pl.multiple_of(lax.rem(z + offset + 8, 8) * 32, 32)
        out_ref[pl.ds(row, 32), :] = ref[:, pl.ds(at, width)]
    row = pl.multiple_of(lax.rem(z + 4, 8) * 32, 32)
    out_ref[pl.ds(row, 16), :] = top[:, pl.ds(at, width)]
    out_ref[pl.ds(pl.multiple_of(row + 16, 16), 16), :] = low[:, pl.ds(at, width)]


def accumulate(z, core, blocks, panels, lhs, acc):
    width = panels[0].shape[1]
    acc[...] = jnp.zeros_like(acc)
    for half in range(2):
        for at in range(0, width, CHUNK):
            collect(z, blocks, half * width + at, CHUNK, lhs)
            for number in range(2):
                ref = panels[2 * number + half]
                other = core if number == 0 else 1 - core
                columns = pl.ds(pl.multiple_of(other * 256, 256), 256)
                acc[:, columns] += lax.dot_general(
                    lhs[...],
                    ref[:, at : at + CHUNK],
                    (((1,), (1,)), ((), ())),
                    preferred_element_type=jnp.float32,
                )


def near_kernel(place_ref, *refs):
    blocks, panels, (out_ref, lhs) = refs[:9], refs[9:13], refs[13:]
    accumulate(place_ref[1], place_ref[2], blocks, panels, lhs, out_ref)


def product_kernel(place_ref, *refs):
    blocks, panels, near_ref = refs[:9], refs[9:13], refs[13]
    turn_ref, home_ref, lhs, far, acc, local = refs[14:]
    xlo, z, core = place_ref[0], place_ref[1], place_ref[2]
    strings = blocks[0].shape[1]
    accumulate(z, core, blocks, panels, lhs, far)
    acc[:, pl.ds(pl.multiple_of(xlo * 512, 512), 512)] = near_ref[...]
    acc[:, pl.ds(pl.multiple_of((1 - xlo) * 512, 512), 512)] = far[...]

    for side in range(2):
        at = pl.multiple_of(side * (strings // 2) + z * 512, 512)
        collect(z, blocks, at, 512, local.at[:, side * 512 : side * 512 + 512])

    coeff = local[...].astype(jnp.float32)
    projection = jnp.sum(2.0 * coeff * acc[...])
    weight = jnp.sum(coeff * coeff)
    lane = lax.broadcasted_iota(jnp.int32, (8, LANES), 1)
    row = lax.broadcasted_iota(jnp.int32, (8, LANES), 0)
    sums = jnp.where(lane == 0, projection, jnp.where(lane == 1, weight, 0.0))
    sums = jnp.where(row == 0, sums, 0.0)
    for there in range(8):
        for part in range(8):
            turn_ref[there, part * 32 : part * 32 + 32, :] = acc[
                there * 32 : there * 32 + 32, part * LANES : part * LANES + LANES
            ]
        turn_ref[there, 256:264, :] = sums
    for target in range(32):
        quarter, col = target // 8, target % 8
        for part in range(2):
            lanes = quarter * 256 + part * LANES
            for below in range(2):
                at = (2 * (col % 4) + below) * 32 + col // 4 * 16
                home_ref[target, part * 32 + below * 16 : part * 32 + below * 16 + 16, :] = acc[
                    at : at + 16, lanes : lanes + LANES
                ]


def multiply_near(place, blocks, panels):
    vmem = pl.BlockSpec(memory_space=pltpu.VMEM)
    return pl.pallas_call(
        near_kernel,
        in_specs=[pl.BlockSpec(memory_space=pltpu.SMEM)] + [vmem] * (len(blocks) + len(panels)),
        out_specs=vmem,
        scratch_shapes=[pltpu.VMEM((256, CHUNK), jnp.bfloat16)],
        out_shape=jax.ShapeDtypeStruct((256, 512), jnp.float32),
        compiler_params=pltpu.CompilerParams(vmem_limit_bytes=20 * MIB),
        cost_estimate=pl.CostEstimate(
            flops=2 * 256 * 512 * NS, bytes_accessed=12 * MIB, transcendentals=0
        ),
    )(place, *blocks, *panels)


def multiply(place, blocks, panels, near):
    vmem = pl.BlockSpec(memory_space=pltpu.VMEM)
    return pl.pallas_call(
        product_kernel,
        in_specs=[pl.BlockSpec(memory_space=pltpu.SMEM)] + [vmem] * (len(blocks) + len(panels) + 1),
        out_specs=[vmem, vmem],
        scratch_shapes=[
            pltpu.VMEM((256, CHUNK), jnp.bfloat16),
            pltpu.VMEM((256, 512), jnp.float32),
            pltpu.VMEM((256, 1024), jnp.float32),
            pltpu.VMEM((256, 1024), jnp.bfloat16),
        ],
        out_shape=[
            jax.ShapeDtypeStruct((8, 264, LANES), jnp.float32),
            jax.ShapeDtypeStruct((32, 64, LANES), jnp.float32),
        ],
        compiler_params=pltpu.CompilerParams(vmem_limit_bytes=24 * MIB),
        cost_estimate=pl.CostEstimate(
            flops=2 * 256 * 512 * NS, bytes_accessed=16 * MIB, transcendentals=0
        ),
    )(place, *blocks, *panels, near)


def split_kernel(value_ref, out_ref, start):
    out_ref[...] = value_ref[start : start + out_ref.shape[0], :]


def take_rows(value, start):
    rows, cols = value.shape
    return pl.pallas_call(
        functools.partial(split_kernel, start=start),
        out_shape=jax.ShapeDtypeStruct((rows // 2, cols), value.dtype),
        compiler_params=pltpu.CompilerParams(vmem_limit_bytes=3 * MIB),
    )(value)


def pack_kernel(turn_ref, home_ref, out_ref):
    sums = jnp.sum(turn_ref[:, 256:264, :], axis=0)
    for target in range(32):
        row, col = target // 8, target % 8
        out_ref[target, 0:64, :] = home_ref[target, :, :]
        for part in range(8):
            source = ((col // 4) * 4 + part % 4) * 32 + row * 8
            out_ref[target, 64 + part * 8 : 72 + part * 8, :] = turn_ref[
                2 * (col % 4) + part // 4, source : source + 8, :
            ]
        out_ref[target, 128:136, :] = sums


def pack(turn, home):
    return pl.pallas_call(
        pack_kernel,
        out_shape=jax.ShapeDtypeStruct((32, 136, LANES), jnp.float32),
        compiler_params=pltpu.CompilerParams(vmem_limit_bytes=16 * MIB),
        cost_estimate=pl.CostEstimate(flops=0, bytes_accessed=5 * MIB, transcendentals=0),
    )(turn, home)


def finish_kernel(update_ref, totals_ref, own_ref, out_ref, stats_ref):
    totals = jnp.sum(totals_ref[...], axis=0, keepdims=True) * (1.0 / (NS * NS))
    lane = lax.broadcasted_iota(jnp.int32, (1, LANES), 1)
    spread = jnp.sum(jnp.where(lane == 0, totals, 0.0), axis=1, keepdims=True)
    out_ref[...] = update_ref[...] * lax.rsqrt(spread + 1e-06)
    stats_ref[...] = jnp.where(lane == 0, own_ref[0:1, :], jnp.sqrt(totals))


def finish(update, totals, own):
    return pl.pallas_call(
        finish_kernel,
        out_shape=[
            jax.ShapeDtypeStruct(update.shape, jnp.float32),
            jax.ShapeDtypeStruct((1, LANES), jnp.float32),
        ],
        compiler_params=pltpu.CompilerParams(vmem_limit_bytes=16 * MIB),
        cost_estimate=pl.CostEstimate(flops=update.size, bytes_accessed=2 * MIB, transcendentals=0),
    )(update, totals, own)


def update_kernel(tiles_ref, coeff_ref, diag_ref, update_ref, sums_ref, theta_ref):
    totals = jnp.sum(tiles_ref[:, 128:136, :], axis=0)
    lane = lax.broadcasted_iota(jnp.int32, (8, LANES), 1)
    projection = jnp.sum(jnp.where(lane == 0, totals, 0.0))
    weight = jnp.sum(jnp.where(lane == 1, totals, 0.0))
    theta = jnp.full((1, 1), projection) / jnp.full((1, 1), weight)
    squares = jnp.zeros((8, LANES), jnp.float32)
    spread = jnp.zeros((8, LANES), jnp.float32)
    for part in range(2):
        rows = slice(part * LANES, part * LANES + LANES)
        for index in range(8):
            cols = slice(index * LANES, index * LANES + LANES)
            quarter, group = index // 2, index % 2
            at = part * 32 + quarter * 8
            straight = tiles_ref[group * 16 : group * 16 + 16, at : at + 8, :]
            straight = straight.reshape(LANES, LANES).T
            turned = tiles_ref[part * 16 : part * 16 + 16, 64 + index * 8 : 72 + index * 8, :]
            turned = turned.reshape(LANES, LANES)
            coeff = coeff_ref[rows, cols].astype(jnp.float32)
            residual = straight + turned - theta * coeff
            update = residual / jnp.maximum(jnp.abs(diag_ref[rows, cols] - theta), 1.0)
            update_ref[rows, cols] = update
            squares += jnp.sum((residual * residual).reshape(16, 8, LANES), axis=0)
            spread += jnp.sum((update * update).reshape(16, 8, LANES), axis=0)
    theta_ref[...] = jnp.broadcast_to(theta, theta_ref.shape)
    values = jnp.where(lane == 0, jnp.sum(spread), jnp.where(lane == 1, jnp.sum(squares), 0.0))
    sums_ref[...] = jnp.broadcast_to(values[0:1, :], sums_ref.shape)


def make_update(tiles, coeff, diagonal):
    return pl.pallas_call(
        update_kernel,
        out_shape=[
            jax.ShapeDtypeStruct(coeff.shape, jnp.float32),
            jax.ShapeDtypeStruct((256, LANES), jnp.float32),
            jax.ShapeDtypeStruct((8, LANES), jnp.float32),
        ],
        compiler_params=pltpu.CompilerParams(vmem_limit_bytes=16 * MIB),
        cost_estimate=pl.CostEstimate(
            flops=10 * coeff.size, bytes_accessed=5 * MIB, transcendentals=0
        ),
    )(tiles, coeff, diagonal)


def swap(value):
    return lax.ppermute(value, "core", [(0, 1), (1, 0)])


def shift(value, step):
    count = lax.axis_size("z")
    return lax.ppermute(value, "z", [(i, (i + step) % count) for i in range(count)])


def shift_x(value, step):
    def index(x):
        return x % 2 * 2 + x // 2

    pairs = [(index(x), index((x + step) % 4)) for x in range(4)]
    return lax.ppermute(value, ("xlo", "xhi"), pairs)


def exchange(value, axes):
    return lax.all_to_all(value, axes, split_axis=0, concat_axis=0, tiled=True)


def body(ham, coeff, tile_mask, occupation, orbital_energy, coulomb):
    rows, strings = ham.shape
    cols = coeff.shape[1]
    core = lax.axis_index("core")
    xlo = lax.axis_index("xlo")
    z = lax.axis_index("z")
    row_index = (xlo * 8 + z) * 2 + core
    col_index = lax.axis_index("xhi") * 4 + lax.axis_index("y")

    place = jnp.stack([xlo, z, core]).astype(jnp.int32)
    ham, place = lax.optimization_barrier((ham, place))
    pair, pair_mask = swap(ham), swap(tile_mask)
    own_a, own_b = mask_half(ham, tile_mask, 0), mask_half(ham, tile_mask, 1)

    block = exchange(coeff.reshape(32, 8, cols), PLANE)
    block = block.reshape(4, 8, 8, cols).transpose(0, 2, 1, 3).reshape(32, strings)
    block, own_a, own_b, pair, pair_mask = lax.optimization_barrier(
        (block, own_a, own_b, pair, pair_mask)
    )
    far_a, far_b = shift_x(own_a, 1), shift_x(own_b, -1)
    p1, m1, pair, pair_mask = lax.optimization_barrier(
        (shift(block, 1), shift(block, -1), pair, pair_mask)
    )
    pair_a = mask_half(pair, pair_mask, 0)
    p2, m2, pair_a = lax.optimization_barrier((shift(p1, 1), shift(m1, -1), pair_a))
    p3, m3 = shift(p2, 1), shift(m2, -1)
    top, low = take_rows(p3, 0), take_rows(m3, 16)
    top, low, pair, pair_mask = lax.optimization_barrier((top, low, pair, pair_mask))
    pair_b = mask_half(pair, pair_mask, 1)
    top, low, pair_b, far_a, far_b = lax.optimization_barrier(
        (shift(top, 1), shift(low, -1), pair_b, far_a, far_b)
    )
    cross_a, cross_b = swap(far_a), swap(far_b)

    blocks = (block, p1, p2, p3, m1, m2, m3, top, low)
    near = multiply_near(place, blocks, (own_a, own_b, pair_a, pair_b))
    turn, home = multiply(place, blocks, (far_a, far_b, cross_a, cross_b), near)

    tiles = exchange(pack(exchange(turn, "z"), home), PLANE)

    occ_float = occupation.astype(jnp.float32)
    occ_alpha = lax.dynamic_slice_in_dim(occ_float, row_index * rows, rows, 1)
    occ_beta = lax.dynamic_slice_in_dim(occ_float, col_index * cols, cols, 1)
    energy_alpha = jnp.dot(orbital_energy, occ_alpha, precision=lax.Precision.HIGHEST)
    energy_beta = jnp.dot(orbital_energy, occ_beta, precision=lax.Precision.HIGHEST)
    coupling = jnp.dot(
        jnp.dot(occ_alpha.T, coulomb, precision=lax.Precision.HIGHEST),
        occ_beta,
        precision=lax.Precision.HIGHEST,
    )
    diagonal = energy_alpha[:, None] + energy_beta[None, :] + coupling

    update, sums, theta = make_update(tiles, coeff, diagonal)
    correction, stats = finish(update, exchange(sums, AXES), theta)
    return (correction, stats[0, :2])


def solution(mesh):
    fine = Mesh(mesh.devices.reshape(SIZES), AXES)
    in_specs = (P(ROW, None), P(ROW, COL), P(ROW, None), P(), P(), P())
    out_specs = (P(ROW, COL), P())
    return jax.shard_map(body, mesh=fine, in_specs=in_specs, out_specs=out_specs, check_vma=False)
```

```python
import functools

import jax
import jax.numpy as jnp
from jax import lax
from jax.experimental import pallas as pl
from jax.experimental.pallas import tpu as pltpu
from jax.sharding import Mesh, PartitionSpec as P

NS = 8192
AXES = ("xlo", "z", "core", "xhi", "y")
SIZES = (2, 8, 2, 2, 4)
ROW = ("xlo", "z", "core")
COL = ("xhi", "y")
PLANE = ("xlo", "core", "xhi", "y")
LANES = 128
CHUNK = 1024
MIB = 1024 * 1024


def mask_kernel(ham_ref, mask_ref, out_ref):
    rows, cols = ham_ref.shape
    mask_rows, mask_cols = mask_ref.shape
    tile = size = rows // mask_rows
    spread = (
        lax.broadcasted_iota(jnp.int32, (mask_cols, cols), 1) // size + pl.program_id(0) * (cols // size)
        == lax.broadcasted_iota(jnp.int32, (mask_cols, cols), 0)
    ).astype(jnp.bfloat16)
    mask = mask_ref[...].astype(jnp.float32).astype(jnp.bfloat16)
    wide = jnp.dot(mask, spread, preferred_element_type=jnp.float32)
    for index in range(mask_rows):
        at = index * tile
        values = ham_ref[at : at + tile, :].astype(jnp.float32) * wide[index : index + 1, :]
        out_ref[at : at + tile, :] = values.astype(jnp.bfloat16)


def mask_half(ham, tile_mask, half):
    rows, cols = ham.shape
    mask_rows, mask_cols = tile_mask.shape
    return pl.pallas_call(
        mask_kernel,
        grid=(4,),
        in_specs=[
            pl.BlockSpec((rows, cols // 8), lambda j: (0, half * 4 + j)),
            pl.BlockSpec((mask_rows, mask_cols // 2), lambda j: (0, half)),
        ],
        out_specs=pl.BlockSpec((rows, cols // 8), lambda j: (0, j)),
        out_shape=jax.ShapeDtypeStruct((rows, cols // 2), jnp.bfloat16),
        compiler_params=pltpu.CompilerParams(vmem_limit_bytes=8 * MIB),
        cost_estimate=pl.CostEstimate(
            flops=rows * cols, bytes_accessed=2 * rows * cols, transcendentals=0
        ),
    )(ham, tile_mask)


def collect(z, blocks, at, width, out_ref):
    c0, p1, p2, p3, m1, m2, m3, top, low = blocks
    for offset, ref in ((0, c0), (-1, p1), (-2, p2), (-3, p3), (1, m1), (2, m2), (3, m3)):
        row = pl.multiple_of(lax.rem(z + offset + 8, 8) * 32, 32)
        out_ref[pl.ds(row, 32), :] = ref[:, pl.ds(at, width)]
    row = pl.multiple_of(lax.rem(z + 4, 8) * 32, 32)
    out_ref[pl.ds(row, 16), :] = top[:, pl.ds(at, width)]
    out_ref[pl.ds(pl.multiple_of(row + 16, 16), 16), :] = low[:, pl.ds(at, width)]


def accumulate(z, blocks, panels, columns, lhs, acc):
    width = panels[0].shape[1]
    acc[...] = jnp.zeros_like(acc)
    for half in range(2):
        for at in range(0, width, CHUNK):
            collect(z, blocks, half * width + at, CHUNK, lhs)
            for number, column in enumerate(columns):
                place = pl.ds(pl.multiple_of(column * 256, 256), 256)
                acc[:, place] += lax.dot_general(
                    lhs[...],
                    panels[2 * number + half][:, at : at + CHUNK],
                    (((1,), (1,)), ((), ())),
                    preferred_element_type=jnp.float32,
                )


def near_kernel(place_ref, *refs):
    blocks, panels, (out_ref, lhs, acc) = refs[:9], refs[9:15], refs[15:]
    core = place_ref[2]
    accumulate(place_ref[1], blocks, panels, (core, 1 - core, jnp.int32(2)), lhs, acc)
    out_ref[...] = acc[...]


def product_kernel(place_ref, *refs):
    blocks, panels, near_ref = refs[:9], refs[9:11], refs[11]
    turn_ref, home_ref, lhs, cross, acc, local = refs[12:]
    xlo, z, core = place_ref[0], place_ref[1], place_ref[2]
    strings = blocks[0].shape[1]
    accumulate(z, blocks, panels, (jnp.int32(0),), lhs, cross)
    acc[:, pl.ds(pl.multiple_of(xlo * 512, 512), 512)] = near_ref[:, 0:512]
    far = (1 - xlo) * 2
    acc[:, pl.ds(pl.multiple_of((far + core) * 256, 256), 256)] = near_ref[:, 512:768]
    acc[:, pl.ds(pl.multiple_of((far + 1 - core) * 256, 256), 256)] = cross[...]

    for side in range(2):
        at = pl.multiple_of(side * (strings // 2) + z * 512, 512)
        collect(z, blocks, at, 512, local.at[:, side * 512 : side * 512 + 512])

    coeff = local[...].astype(jnp.float32)
    projection = jnp.sum(2.0 * coeff * acc[...])
    weight = jnp.sum(coeff * coeff)
    lane = lax.broadcasted_iota(jnp.int32, (8, LANES), 1)
    row = lax.broadcasted_iota(jnp.int32, (8, LANES), 0)
    sums = jnp.where(lane == 0, projection, jnp.where(lane == 1, weight, 0.0))
    sums = jnp.where(row == 0, sums, 0.0)
    for there in range(8):
        for part in range(8):
            turn_ref[there, part * 32 : part * 32 + 32, :] = acc[
                there * 32 : there * 32 + 32, part * LANES : part * LANES + LANES
            ]
        turn_ref[there, 256:264, :] = sums
    for target in range(32):
        quarter, col = target // 8, target % 8
        for part in range(2):
            lanes = quarter * 256 + part * LANES
            for below in range(2):
                at = (2 * (col % 4) + below) * 32 + col // 4 * 16
                home_ref[target, part * 32 + below * 16 : part * 32 + below * 16 + 16, :] = acc[
                    at : at + 16, lanes : lanes + LANES
                ]


def multiply_near(place, blocks, panels):
    vmem = pl.BlockSpec(memory_space=pltpu.VMEM)
    return pl.pallas_call(
        near_kernel,
        in_specs=[pl.BlockSpec(memory_space=pltpu.SMEM)] + [vmem] * (len(blocks) + len(panels)),
        out_specs=vmem,
        scratch_shapes=[
            pltpu.VMEM((256, CHUNK), jnp.bfloat16),
            pltpu.VMEM((256, 768), jnp.float32),
        ],
        out_shape=jax.ShapeDtypeStruct((256, 768), jnp.float32),
        compiler_params=pltpu.CompilerParams(vmem_limit_bytes=20 * MIB),
        cost_estimate=pl.CostEstimate(
            flops=2 * 256 * 768 * NS, bytes_accessed=16 * MIB, transcendentals=0
        ),
    )(place, *blocks, *panels)


def multiply(place, blocks, panels, near):
    vmem = pl.BlockSpec(memory_space=pltpu.VMEM)
    return pl.pallas_call(
        product_kernel,
        in_specs=[pl.BlockSpec(memory_space=pltpu.SMEM)] + [vmem] * (len(blocks) + len(panels) + 1),
        out_specs=[vmem, vmem],
        scratch_shapes=[
            pltpu.VMEM((256, CHUNK), jnp.bfloat16),
            pltpu.VMEM((256, 256), jnp.float32),
            pltpu.VMEM((256, 1024), jnp.float32),
            pltpu.VMEM((256, 1024), jnp.bfloat16),
        ],
        out_shape=[
            jax.ShapeDtypeStruct((8, 264, LANES), jnp.float32),
            jax.ShapeDtypeStruct((32, 64, LANES), jnp.float32),
        ],
        compiler_params=pltpu.CompilerParams(vmem_limit_bytes=24 * MIB),
        cost_estimate=pl.CostEstimate(
            flops=2 * 256 * 256 * NS, bytes_accessed=12 * MIB, transcendentals=0
        ),
    )(place, *blocks, *panels, near)


def split_kernel(value_ref, out_ref, start):
    out_ref[...] = value_ref[start : start + out_ref.shape[0], :]


def take_rows(value, start):
    rows, cols = value.shape
    return pl.pallas_call(
        functools.partial(split_kernel, start=start),
        out_shape=jax.ShapeDtypeStruct((rows // 2, cols), value.dtype),
        compiler_params=pltpu.CompilerParams(vmem_limit_bytes=3 * MIB),
    )(value)


def pack_kernel(turn_ref, home_ref, out_ref):
    sums = jnp.sum(turn_ref[:, 256:264, :], axis=0)
    for target in range(32):
        row, col = target // 8, target % 8
        out_ref[target, 0:64, :] = home_ref[target, :, :]
        for part in range(8):
            source = ((col // 4) * 4 + part % 4) * 32 + row * 8
            out_ref[target, 64 + part * 8 : 72 + part * 8, :] = turn_ref[
                2 * (col % 4) + part // 4, source : source + 8, :
            ]
        out_ref[target, 128:136, :] = sums


def pack(turn, home):
    return pl.pallas_call(
        pack_kernel,
        out_shape=jax.ShapeDtypeStruct((32, 136, LANES), jnp.float32),
        compiler_params=pltpu.CompilerParams(vmem_limit_bytes=16 * MIB),
        cost_estimate=pl.CostEstimate(flops=0, bytes_accessed=5 * MIB, transcendentals=0),
    )(turn, home)


def finish_kernel(update_ref, totals_ref, own_ref, out_ref, stats_ref):
    totals = jnp.sum(totals_ref[...], axis=0, keepdims=True) * (1.0 / (NS * NS))
    lane = lax.broadcasted_iota(jnp.int32, (1, LANES), 1)
    spread = jnp.sum(jnp.where(lane == 0, totals, 0.0), axis=1, keepdims=True)
    out_ref[...] = update_ref[...] * lax.rsqrt(spread + 1e-06)
    stats_ref[...] = jnp.where(lane == 0, own_ref[0:1, :], jnp.sqrt(totals))


def finish(update, totals, own):
    return pl.pallas_call(
        finish_kernel,
        out_shape=[
            jax.ShapeDtypeStruct(update.shape, jnp.float32),
            jax.ShapeDtypeStruct((1, LANES), jnp.float32),
        ],
        compiler_params=pltpu.CompilerParams(vmem_limit_bytes=16 * MIB),
        cost_estimate=pl.CostEstimate(flops=update.size, bytes_accessed=2 * MIB, transcendentals=0),
    )(update, totals, own)


def update_kernel(tiles_ref, coeff_ref, diag_ref, update_ref, sums_ref, theta_ref):
    totals = jnp.sum(tiles_ref[:, 128:136, :], axis=0)
    lane = lax.broadcasted_iota(jnp.int32, (8, LANES), 1)
    projection = jnp.sum(jnp.where(lane == 0, totals, 0.0))
    weight = jnp.sum(jnp.where(lane == 1, totals, 0.0))
    theta = jnp.full((1, 1), projection) / jnp.full((1, 1), weight)
    squares = jnp.zeros((8, LANES), jnp.float32)
    spread = jnp.zeros((8, LANES), jnp.float32)
    for part in range(2):
        rows = slice(part * LANES, part * LANES + LANES)
        for index in range(8):
            cols = slice(index * LANES, index * LANES + LANES)
            quarter, group = index // 2, index % 2
            at = part * 32 + quarter * 8
            straight = tiles_ref[group * 16 : group * 16 + 16, at : at + 8, :]
            straight = straight.reshape(LANES, LANES).T
            turned = tiles_ref[part * 16 : part * 16 + 16, 64 + index * 8 : 72 + index * 8, :]
            turned = turned.reshape(LANES, LANES)
            coeff = coeff_ref[rows, cols].astype(jnp.float32)
            residual = straight + turned - theta * coeff
            update = residual / jnp.maximum(jnp.abs(diag_ref[rows, cols] - theta), 1.0)
            update_ref[rows, cols] = update
            squares += jnp.sum((residual * residual).reshape(16, 8, LANES), axis=0)
            spread += jnp.sum((update * update).reshape(16, 8, LANES), axis=0)
    theta_ref[...] = jnp.broadcast_to(theta, theta_ref.shape)
    values = jnp.where(lane == 0, jnp.sum(spread), jnp.where(lane == 1, jnp.sum(squares), 0.0))
    sums_ref[...] = jnp.broadcast_to(values[0:1, :], sums_ref.shape)


def make_update(tiles, coeff, diagonal):
    return pl.pallas_call(
        update_kernel,
        out_shape=[
            jax.ShapeDtypeStruct(coeff.shape, jnp.float32),
            jax.ShapeDtypeStruct((256, LANES), jnp.float32),
            jax.ShapeDtypeStruct((8, LANES), jnp.float32),
        ],
        compiler_params=pltpu.CompilerParams(vmem_limit_bytes=16 * MIB),
        cost_estimate=pl.CostEstimate(
            flops=10 * coeff.size, bytes_accessed=5 * MIB, transcendentals=0
        ),
    )(tiles, coeff, diagonal)


def swap(value):
    return lax.ppermute(value, "core", [(0, 1), (1, 0)])


def shift(value, step):
    count = lax.axis_size("z")
    return lax.ppermute(value, "z", [(i, (i + step) % count) for i in range(count)])


def shift_x(value, step):
    def index(x):
        return x % 2 * 2 + x // 2

    pairs = [(index(x), index((x + step) % 4)) for x in range(4)]
    return lax.ppermute(value, ("xlo", "xhi"), pairs)


def exchange(value, axes):
    return lax.all_to_all(value, axes, split_axis=0, concat_axis=0, tiled=True)


def body(ham, coeff, tile_mask, occupation, orbital_energy, coulomb):
    rows, strings = ham.shape
    cols = coeff.shape[1]
    core = lax.axis_index("core")
    xlo = lax.axis_index("xlo")
    z = lax.axis_index("z")
    row_index = (xlo * 8 + z) * 2 + core
    col_index = lax.axis_index("xhi") * 4 + lax.axis_index("y")

    place = jnp.stack([xlo, z, core]).astype(jnp.int32)
    ham, place = lax.optimization_barrier((ham, place))
    pair, pair_mask = swap(ham), swap(tile_mask)
    own_a, own_b = mask_half(ham, tile_mask, 0), mask_half(ham, tile_mask, 1)

    block = exchange(coeff.reshape(32, 8, cols), PLANE)
    block = block.reshape(4, 8, 8, cols).transpose(0, 2, 1, 3).reshape(32, strings)
    block, own_a, own_b, pair, pair_mask = lax.optimization_barrier(
        (block, own_a, own_b, pair, pair_mask)
    )
    far_a, far_b = shift_x(own_a, 1), shift_x(own_b, -1)
    p1, m1, pair, pair_mask = lax.optimization_barrier(
        (shift(block, 1), shift(block, -1), pair, pair_mask)
    )
    pair_a = mask_half(pair, pair_mask, 0)
    p2, m2, pair_a = lax.optimization_barrier((shift(p1, 1), shift(m1, -1), pair_a))
    p3, m3 = shift(p2, 1), shift(m2, -1)
    top, low = take_rows(p3, 0), take_rows(m3, 16)
    top, low, pair, pair_mask = lax.optimization_barrier((top, low, pair, pair_mask))
    pair_b = mask_half(pair, pair_mask, 1)
    top, low, pair_b, far_a, far_b = lax.optimization_barrier(
        (shift(top, 1), shift(low, -1), pair_b, far_a, far_b)
    )
    cross_a, cross_b = swap(far_a), swap(far_b)

    blocks = (block, p1, p2, p3, m1, m2, m3, top, low)
    near = multiply_near(place, blocks, (own_a, own_b, pair_a, pair_b, far_a, far_b))
    turn, home = multiply(place, blocks, (cross_a, cross_b), near)

    tiles = exchange(pack(exchange(turn, "z"), home), PLANE)

    occ_float = occupation.astype(jnp.float32)
    occ_alpha = lax.dynamic_slice_in_dim(occ_float, row_index * rows, rows, 1)
    occ_beta = lax.dynamic_slice_in_dim(occ_float, col_index * cols, cols, 1)
    energy_alpha = jnp.dot(orbital_energy, occ_alpha, precision=lax.Precision.HIGHEST)
    energy_beta = jnp.dot(orbital_energy, occ_beta, precision=lax.Precision.HIGHEST)
    coupling = jnp.dot(
        jnp.dot(occ_alpha.T, coulomb, precision=lax.Precision.HIGHEST),
        occ_beta,
        precision=lax.Precision.HIGHEST,
    )
    diagonal = energy_alpha[:, None] + energy_beta[None, :] + coupling

    update, sums, theta = make_update(tiles, coeff, diagonal)
    correction, stats = finish(update, exchange(sums, AXES), theta)
    return (correction, stats[0, :2])


def solution(mesh):
    fine = Mesh(mesh.devices.reshape(SIZES), AXES)
    in_specs = (P(ROW, None), P(ROW, COL), P(ROW, None), P(), P(), P())
    out_specs = (P(ROW, COL), P())
    return jax.shard_map(body, mesh=fine, in_specs=in_specs, out_specs=out_specs, check_vma=False)
```

```python
import functools

import jax
import jax.numpy as jnp
from jax import lax
from jax.experimental import pallas as pl
from jax.experimental.pallas import tpu as pltpu
from jax.sharding import Mesh, PartitionSpec as P

NS = 8192
AXES = ("xlo", "z", "core", "xhi", "y")
SIZES = (2, 8, 2, 2, 4)
ROW = ("xlo", "z", "core")
COL = ("xhi", "y")
PLANE = ("xlo", "core", "xhi", "y")
LANES = 128
CHUNK = 1024
MIB = 1024 * 1024


def mask_kernel(ham_ref, mask_ref, out_ref):
    rows, cols = ham_ref.shape
    mask_rows, mask_cols = mask_ref.shape
    tile = size = rows // mask_rows
    spread = (
        lax.broadcasted_iota(jnp.int32, (mask_cols, cols), 1) // size + pl.program_id(0) * (cols // size)
        == lax.broadcasted_iota(jnp.int32, (mask_cols, cols), 0)
    ).astype(jnp.bfloat16)
    mask = mask_ref[...].astype(jnp.float32).astype(jnp.bfloat16)
    wide = jnp.dot(mask, spread, preferred_element_type=jnp.float32)
    for index in range(mask_rows):
        at = index * tile
        values = ham_ref[at : at + tile, :].astype(jnp.float32) * wide[index : index + 1, :]
        out_ref[at : at + tile, :] = values.astype(jnp.bfloat16)


def mask_half(ham, tile_mask, half):
    rows, cols = ham.shape
    mask_rows, mask_cols = tile_mask.shape
    return pl.pallas_call(
        mask_kernel,
        grid=(4,),
        in_specs=[
            pl.BlockSpec((rows, cols // 8), lambda j: (0, half * 4 + j)),
            pl.BlockSpec((mask_rows, mask_cols // 2), lambda j: (0, half)),
        ],
        out_specs=pl.BlockSpec((rows, cols // 8), lambda j: (0, j)),
        out_shape=jax.ShapeDtypeStruct((rows, cols // 2), jnp.bfloat16),
        compiler_params=pltpu.CompilerParams(vmem_limit_bytes=8 * MIB),
        cost_estimate=pl.CostEstimate(
            flops=rows * cols, bytes_accessed=2 * rows * cols, transcendentals=0
        ),
    )(ham, tile_mask)


def collect(z, blocks, at, width, out_ref):
    c0, p1, p2, p3, m1, m2, m3, top, low = blocks
    for offset, ref in ((0, c0), (-1, p1), (-2, p2), (-3, p3), (1, m1), (2, m2), (3, m3)):
        row = pl.multiple_of(lax.rem(z + offset + 8, 8) * 32, 32)
        out_ref[pl.ds(row, 32), :] = ref[:, pl.ds(at, width)]
    row = pl.multiple_of(lax.rem(z + 4, 8) * 32, 32)
    out_ref[pl.ds(row, 16), :] = top[:, pl.ds(at, width)]
    out_ref[pl.ds(pl.multiple_of(row + 16, 16), 16), :] = low[:, pl.ds(at, width)]


def accumulate(z, blocks, panels, columns, lhs, acc):
    width = panels[0].shape[1]
    acc[...] = jnp.zeros_like(acc)
    for half in range(2):
        for at in range(0, width, CHUNK):
            collect(z, blocks, half * width + at, CHUNK, lhs)
            for number, column in enumerate(columns):
                place = pl.ds(pl.multiple_of(column * 256, 256), 256)
                acc[:, place] += lax.dot_general(
                    lhs[...],
                    panels[2 * number + half][:, at : at + CHUNK],
                    (((1,), (1,)), ((), ())),
                    preferred_element_type=jnp.float32,
                )


def near_kernel(place_ref, *refs):
    blocks, panels, (out_ref, lhs, acc) = refs[:9], refs[9:15], refs[15:]
    core = place_ref[2]
    accumulate(place_ref[1], blocks, panels, (core, 1 - core, jnp.int32(2)), lhs, acc)
    out_ref[...] = acc[...]


def product_kernel(place_ref, *refs):
    blocks, panels, near_ref = refs[:9], refs[9:11], refs[11]
    turn_ref, home_ref, lhs, cross, acc, local = refs[12:]
    xlo, z, core = place_ref[0], place_ref[1], place_ref[2]
    strings = blocks[0].shape[1]
    accumulate(z, blocks, panels, (jnp.int32(0),), lhs, cross)
    acc[:, pl.ds(pl.multiple_of(xlo * 512, 512), 512)] = near_ref[:, 0:512]
    far = (1 - xlo) * 2
    acc[:, pl.ds(pl.multiple_of((far + core) * 256, 256), 256)] = near_ref[:, 512:768]
    acc[:, pl.ds(pl.multiple_of((far + 1 - core) * 256, 256), 256)] = cross[...]

    for side in range(2):
        at = pl.multiple_of(side * (strings // 2) + z * 512, 512)
        collect(z, blocks, at, 512, local.at[:, side * 512 : side * 512 + 512])

    coeff = local[...].astype(jnp.float32)
    projection = jnp.sum(2.0 * coeff * acc[...])
    weight = jnp.sum(coeff * coeff)
    lane = lax.broadcasted_iota(jnp.int32, (8, LANES), 1)
    row = lax.broadcasted_iota(jnp.int32, (8, LANES), 0)
    sums = jnp.where(lane == 0, projection, jnp.where(lane == 1, weight, 0.0))
    sums = jnp.where(row == 0, sums, 0.0)
    for there in range(8):
        for part in range(8):
            turn_ref[there, part * 32 : part * 32 + 32, :] = acc[
                there * 32 : there * 32 + 32, part * LANES : part * LANES + LANES
            ]
        turn_ref[there, 256:264, :] = sums
    for target in range(32):
        quarter, col = target // 8, target % 8
        for part in range(2):
            lanes = quarter * 256 + part * LANES
            for below in range(2):
                at = (2 * (col % 4) + below) * 32 + col // 4 * 16
                home_ref[target, part * 32 + below * 16 : part * 32 + below * 16 + 16, :] = acc[
                    at : at + 16, lanes : lanes + LANES
                ]


def multiply_near(place, blocks, panels):
    vmem = pl.BlockSpec(memory_space=pltpu.VMEM)
    return pl.pallas_call(
        near_kernel,
        in_specs=[pl.BlockSpec(memory_space=pltpu.SMEM)] + [vmem] * (len(blocks) + len(panels)),
        out_specs=vmem,
        scratch_shapes=[
            pltpu.VMEM((256, CHUNK), jnp.bfloat16),
            pltpu.VMEM((256, 768), jnp.float32),
        ],
        out_shape=jax.ShapeDtypeStruct((256, 768), jnp.float32),
        compiler_params=pltpu.CompilerParams(vmem_limit_bytes=20 * MIB),
        cost_estimate=pl.CostEstimate(
            flops=2 * 256 * 768 * NS, bytes_accessed=16 * MIB, transcendentals=0
        ),
    )(place, *blocks, *panels)


def multiply(place, blocks, panels, near):
    vmem = pl.BlockSpec(memory_space=pltpu.VMEM)
    return pl.pallas_call(
        product_kernel,
        in_specs=[pl.BlockSpec(memory_space=pltpu.SMEM)] + [vmem] * (len(blocks) + len(panels) + 1),
        out_specs=[vmem, vmem],
        scratch_shapes=[
            pltpu.VMEM((256, CHUNK), jnp.bfloat16),
            pltpu.VMEM((256, 256), jnp.float32),
            pltpu.VMEM((256, 1024), jnp.float32),
            pltpu.VMEM((256, 1024), jnp.bfloat16),
        ],
        out_shape=[
            jax.ShapeDtypeStruct((8, 264, LANES), jnp.float32),
            jax.ShapeDtypeStruct((32, 64, LANES), jnp.float32),
        ],
        compiler_params=pltpu.CompilerParams(vmem_limit_bytes=24 * MIB),
        cost_estimate=pl.CostEstimate(
            flops=2 * 256 * 256 * NS, bytes_accessed=12 * MIB, transcendentals=0
        ),
    )(place, *blocks, *panels, near)


def split_kernel(value_ref, out_ref, start):
    out_ref[...] = value_ref[start : start + out_ref.shape[0], :]


def take_rows(value, start):
    rows, cols = value.shape
    return pl.pallas_call(
        functools.partial(split_kernel, start=start),
        out_shape=jax.ShapeDtypeStruct((rows // 2, cols), value.dtype),
        compiler_params=pltpu.CompilerParams(vmem_limit_bytes=3 * MIB),
    )(value)


def pack_kernel(turn_ref, home_ref, out_ref):
    sums = jnp.sum(turn_ref[:, 256:264, :], axis=0)
    for target in range(32):
        row, col = target // 8, target % 8
        out_ref[target, 0:64, :] = home_ref[target, :, :]
        for part in range(8):
            source = ((col // 4) * 4 + part % 4) * 32 + row * 8
            out_ref[target, 64 + part * 8 : 72 + part * 8, :] = turn_ref[
                2 * (col % 4) + part // 4, source : source + 8, :
            ]
        out_ref[target, 128:136, :] = sums


def pack(turn, home):
    return pl.pallas_call(
        pack_kernel,
        out_shape=jax.ShapeDtypeStruct((32, 136, LANES), jnp.float32),
        compiler_params=pltpu.CompilerParams(vmem_limit_bytes=16 * MIB),
        cost_estimate=pl.CostEstimate(flops=0, bytes_accessed=5 * MIB, transcendentals=0),
    )(turn, home)


def finish_kernel(update_ref, totals_ref, own_ref, out_ref, stats_ref):
    totals = jnp.sum(totals_ref[...], axis=0, keepdims=True) * (1.0 / (NS * NS))
    lane = lax.broadcasted_iota(jnp.int32, (1, LANES), 1)
    spread = jnp.sum(jnp.where(lane == 0, totals, 0.0), axis=1, keepdims=True)
    out_ref[...] = update_ref[...] * lax.rsqrt(spread + 1e-06)
    stats_ref[...] = jnp.where(lane == 0, own_ref[0:1, :], jnp.sqrt(totals))


def finish(update, totals, own):
    return pl.pallas_call(
        finish_kernel,
        out_shape=[
            jax.ShapeDtypeStruct(update.shape, jnp.float32),
            jax.ShapeDtypeStruct((1, LANES), jnp.float32),
        ],
        compiler_params=pltpu.CompilerParams(vmem_limit_bytes=16 * MIB),
        cost_estimate=pl.CostEstimate(flops=update.size, bytes_accessed=2 * MIB, transcendentals=0),
    )(update, totals, own)


def update_kernel(tiles_ref, coeff_ref, diag_ref, update_ref, sums_ref, theta_ref):
    totals = jnp.sum(tiles_ref[:, 128:136, :], axis=0)
    lane = lax.broadcasted_iota(jnp.int32, (8, LANES), 1)
    projection = jnp.sum(jnp.where(lane == 0, totals, 0.0))
    weight = jnp.sum(jnp.where(lane == 1, totals, 0.0))
    theta = jnp.full((1, 1), projection) / jnp.full((1, 1), weight)
    squares = jnp.zeros((8, LANES), jnp.float32)
    spread = jnp.zeros((8, LANES), jnp.float32)
    for part in range(2):
        rows = slice(part * LANES, part * LANES + LANES)
        for index in range(8):
            cols = slice(index * LANES, index * LANES + LANES)
            quarter, group = index // 2, index % 2
            at = part * 32 + quarter * 8
            straight = tiles_ref[group * 16 : group * 16 + 16, at : at + 8, :]
            straight = straight.reshape(LANES, LANES).T
            turned = tiles_ref[part * 16 : part * 16 + 16, 64 + index * 8 : 72 + index * 8, :]
            turned = turned.reshape(LANES, LANES)
            coeff = coeff_ref[rows, cols].astype(jnp.float32)
            residual = straight + turned - theta * coeff
            update = residual / jnp.maximum(jnp.abs(diag_ref[rows, cols] - theta), 1.0)
            update_ref[rows, cols] = update
            squares += jnp.sum((residual * residual).reshape(16, 8, LANES), axis=0)
            spread += jnp.sum((update * update).reshape(16, 8, LANES), axis=0)
    theta_ref[...] = jnp.broadcast_to(theta, theta_ref.shape)
    values = jnp.where(lane == 0, jnp.sum(spread), jnp.where(lane == 1, jnp.sum(squares), 0.0))
    sums_ref[...] = jnp.broadcast_to(values[0:1, :], sums_ref.shape)


def make_update(tiles, coeff, diagonal):
    return pl.pallas_call(
        update_kernel,
        out_shape=[
            jax.ShapeDtypeStruct(coeff.shape, jnp.float32),
            jax.ShapeDtypeStruct((256, LANES), jnp.float32),
            jax.ShapeDtypeStruct((8, LANES), jnp.float32),
        ],
        compiler_params=pltpu.CompilerParams(vmem_limit_bytes=16 * MIB),
        cost_estimate=pl.CostEstimate(
            flops=10 * coeff.size, bytes_accessed=5 * MIB, transcendentals=0
        ),
    )(tiles, coeff, diagonal)


def swap(value):
    return lax.ppermute(value, "core", [(0, 1), (1, 0)])


def shift(value, step):
    count = lax.axis_size("z")
    return lax.ppermute(value, "z", [(i, (i + step) % count) for i in range(count)])


def shift_x(value, step):
    def index(x):
        return x % 2 * 2 + x // 2

    pairs = [(index(x), index((x + step) % 4)) for x in range(4)]
    return lax.ppermute(value, ("xlo", "xhi"), pairs)


def exchange(value, axes):
    return lax.all_to_all(value, axes, split_axis=0, concat_axis=0, tiled=True)


def body(ham, coeff, tile_mask, occupation, orbital_energy, coulomb):
    rows, strings = ham.shape
    cols = coeff.shape[1]
    core = lax.axis_index("core")
    xlo = lax.axis_index("xlo")
    z = lax.axis_index("z")
    row_index = (xlo * 8 + z) * 2 + core
    col_index = lax.axis_index("xhi") * 4 + lax.axis_index("y")

    place = jnp.stack([xlo, z, core]).astype(jnp.int32)
    ham, place = lax.optimization_barrier((ham, place))
    pair, pair_mask = swap(ham), swap(tile_mask)
    own_a, own_b = mask_half(ham, tile_mask, 0), mask_half(ham, tile_mask, 1)

    block = exchange(coeff.reshape(32, 8, cols), PLANE)
    block = block.reshape(4, 8, 8, cols).transpose(0, 2, 1, 3).reshape(32, strings)
    block, own_a, own_b, pair, pair_mask = lax.optimization_barrier(
        (block, own_a, own_b, pair, pair_mask)
    )
    far_a, far_b = shift_x(own_a, 1), shift_x(own_b, -1)
    p1, pair, pair_mask = lax.optimization_barrier((shift(block, 1), pair, pair_mask))
    m1 = shift(block, -1)
    pair_a = mask_half(pair, pair_mask, 0)
    p2, pair_a = lax.optimization_barrier((shift(p1, 1), pair_a))
    m2 = shift(m1, -1)
    p3, m3 = shift(p2, 1), shift(m2, -1)
    top, low = take_rows(p3, 0), take_rows(m3, 16)
    top, low, pair, pair_mask = lax.optimization_barrier((top, low, pair, pair_mask))
    pair_b = mask_half(pair, pair_mask, 1)
    top, low, pair_b, far_a, far_b = lax.optimization_barrier(
        (shift(top, 1), shift(low, -1), pair_b, far_a, far_b)
    )
    cross_a, cross_b = swap(far_a), swap(far_b)

    blocks = (block, p1, p2, p3, m1, m2, m3, top, low)
    near = multiply_near(place, blocks, (own_a, own_b, pair_a, pair_b, far_a, far_b))
    turn, home = multiply(place, blocks, (cross_a, cross_b), near)

    tiles = exchange(pack(exchange(turn, "z"), home), PLANE)

    occ_float = occupation.astype(jnp.float32)
    occ_alpha = lax.dynamic_slice_in_dim(occ_float, row_index * rows, rows, 1)
    occ_beta = lax.dynamic_slice_in_dim(occ_float, col_index * cols, cols, 1)
    energy_alpha = jnp.dot(orbital_energy, occ_alpha, precision=lax.Precision.HIGHEST)
    energy_beta = jnp.dot(orbital_energy, occ_beta, precision=lax.Precision.HIGHEST)
    coupling = jnp.dot(
        jnp.dot(occ_alpha.T, coulomb, precision=lax.Precision.HIGHEST),
        occ_beta,
        precision=lax.Precision.HIGHEST,
    )
    diagonal = energy_alpha[:, None] + energy_beta[None, :] + coupling

    update, sums, theta = make_update(tiles, coeff, diagonal)
    correction, stats = finish(update, exchange(sums, AXES), theta)
    return (correction, stats[0, :2])


def solution(mesh):
    fine = Mesh(mesh.devices.reshape(SIZES), AXES)
    in_specs = (P(ROW, None), P(ROW, COL), P(ROW, None), P(), P(), P())
    out_specs = (P(ROW, COL), P())
    return jax.shard_map(body, mesh=fine, in_specs=in_specs, out_specs=out_specs, check_vma=False)
```

```python
import functools

import jax
import jax.numpy as jnp
from jax import lax
from jax.experimental import pallas as pl
from jax.experimental.pallas import tpu as pltpu
from jax.sharding import Mesh, PartitionSpec as P

NS = 8192
AXES = ("xlo", "z", "core", "xhi", "y")
SIZES = (2, 8, 2, 2, 4)
ROW = ("xlo", "z", "core")
COL = ("xhi", "y")
PLANE = ("xlo", "core", "xhi", "y")
LANES = 128
CHUNK = 1024
MIB = 1024 * 1024


def mask_kernel(ham_ref, mask_ref, out_ref):
    rows, cols = ham_ref.shape
    mask_rows, mask_cols = mask_ref.shape
    tile = size = rows // mask_rows
    spread = (
        lax.broadcasted_iota(jnp.int32, (mask_cols, cols), 1) // size + pl.program_id(0) * (cols // size)
        == lax.broadcasted_iota(jnp.int32, (mask_cols, cols), 0)
    ).astype(jnp.bfloat16)
    mask = mask_ref[...].astype(jnp.float32).astype(jnp.bfloat16)
    wide = jnp.dot(mask, spread, preferred_element_type=jnp.float32)
    for index in range(mask_rows):
        at = index * tile
        values = ham_ref[at : at + tile, :].astype(jnp.float32) * wide[index : index + 1, :]
        out_ref[at : at + tile, :] = values.astype(jnp.bfloat16)


def mask_half(ham, tile_mask, half):
    rows, cols = ham.shape
    mask_rows, mask_cols = tile_mask.shape
    return pl.pallas_call(
        mask_kernel,
        grid=(4,),
        in_specs=[
            pl.BlockSpec((rows, cols // 8), lambda j: (0, half * 4 + j)),
            pl.BlockSpec((mask_rows, mask_cols // 2), lambda j: (0, half)),
        ],
        out_specs=pl.BlockSpec((rows, cols // 8), lambda j: (0, j)),
        out_shape=jax.ShapeDtypeStruct((rows, cols // 2), jnp.bfloat16),
        compiler_params=pltpu.CompilerParams(vmem_limit_bytes=8 * MIB),
        cost_estimate=pl.CostEstimate(
            flops=rows * cols, bytes_accessed=2 * rows * cols, transcendentals=0
        ),
    )(ham, tile_mask)


def collect(z, blocks, at, width, out_ref):
    c0, p1, p2, p3, m1, m2, m3, top, low = blocks
    for offset, ref in ((0, c0), (-1, p1), (-2, p2), (-3, p3), (1, m1), (2, m2), (3, m3)):
        row = pl.multiple_of(lax.rem(z + offset + 8, 8) * 32, 32)
        out_ref[pl.ds(row, 32), :] = ref[:, pl.ds(at, width)]
    row = pl.multiple_of(lax.rem(z + 4, 8) * 32, 32)
    out_ref[pl.ds(row, 16), :] = top[:, pl.ds(at, width)]
    out_ref[pl.ds(pl.multiple_of(row + 16, 16), 16), :] = low[:, pl.ds(at, width)]


def accumulate(z, blocks, panels, columns, lhs, acc):
    width = panels[0].shape[1]
    acc[...] = jnp.zeros_like(acc)
    for half in range(2):
        for at in range(0, width, CHUNK):
            collect(z, blocks, half * width + at, CHUNK, lhs)
            for number, column in enumerate(columns):
                place = pl.ds(pl.multiple_of(column * 256, 256), 256)
                acc[:, place] += lax.dot_general(
                    lhs[...],
                    panels[2 * number + half][:, at : at + CHUNK],
                    (((1,), (1,)), ((), ())),
                    preferred_element_type=jnp.float32,
                )


def near_kernel(place_ref, *refs):
    blocks, panels, (out_ref, lhs, acc) = refs[:9], refs[9:15], refs[15:]
    core = place_ref[2]
    accumulate(place_ref[1], blocks, panels, (core, 1 - core, jnp.int32(2)), lhs, acc)
    out_ref[...] = acc[...]


def product_kernel(place_ref, *refs):
    blocks, panels, near_ref = refs[:9], refs[9:11], refs[11]
    turn_ref, home_ref, lhs, cross, acc, local = refs[12:]
    xlo, z, core = place_ref[0], place_ref[1], place_ref[2]
    strings = blocks[0].shape[1]
    accumulate(z, blocks, panels, (jnp.int32(0),), lhs, cross)
    acc[:, pl.ds(pl.multiple_of(xlo * 512, 512), 512)] = near_ref[:, 0:512]
    far = (1 - xlo) * 2
    acc[:, pl.ds(pl.multiple_of((far + core) * 256, 256), 256)] = near_ref[:, 512:768]
    acc[:, pl.ds(pl.multiple_of((far + 1 - core) * 256, 256), 256)] = cross[...]

    for side in range(2):
        at = pl.multiple_of(side * (strings // 2) + z * 512, 512)
        collect(z, blocks, at, 512, local.at[:, side * 512 : side * 512 + 512])

    coeff = local[...].astype(jnp.float32)
    projection = jnp.sum(2.0 * coeff * acc[...])
    weight = jnp.sum(coeff * coeff)
    lane = lax.broadcasted_iota(jnp.int32, (8, LANES), 1)
    row = lax.broadcasted_iota(jnp.int32, (8, LANES), 0)
    sums = jnp.where(lane == 0, projection, jnp.where(lane == 1, weight, 0.0))
    sums = jnp.where(row == 0, sums, 0.0)
    for there in range(8):
        for part in range(8):
            turn_ref[there, part * 32 : part * 32 + 32, :] = acc[
                there * 32 : there * 32 + 32, part * LANES : part * LANES + LANES
            ]
        turn_ref[there, 256:264, :] = sums
    for target in range(32):
        quarter, col = target // 8, target % 8
        for part in range(2):
            lanes = quarter * 256 + part * LANES
            for below in range(2):
                at = (2 * (col % 4) + below) * 32 + col // 4 * 16
                home_ref[target, part * 32 + below * 16 : part * 32 + below * 16 + 16, :] = acc[
                    at : at + 16, lanes : lanes + LANES
                ]


def multiply_near(place, blocks, panels):
    vmem = pl.BlockSpec(memory_space=pltpu.VMEM)
    return pl.pallas_call(
        near_kernel,
        in_specs=[pl.BlockSpec(memory_space=pltpu.SMEM)] + [vmem] * (len(blocks) + len(panels)),
        out_specs=vmem,
        scratch_shapes=[
            pltpu.VMEM((256, CHUNK), jnp.bfloat16),
            pltpu.VMEM((256, 768), jnp.float32),
        ],
        out_shape=jax.ShapeDtypeStruct((256, 768), jnp.float32),
        compiler_params=pltpu.CompilerParams(vmem_limit_bytes=20 * MIB),
        cost_estimate=pl.CostEstimate(
            flops=2 * 256 * 768 * NS, bytes_accessed=16 * MIB, transcendentals=0
        ),
    )(place, *blocks, *panels)


def multiply(place, blocks, panels, near):
    vmem = pl.BlockSpec(memory_space=pltpu.VMEM)
    return pl.pallas_call(
        product_kernel,
        in_specs=[pl.BlockSpec(memory_space=pltpu.SMEM)] + [vmem] * (len(blocks) + len(panels) + 1),
        out_specs=[vmem, vmem],
        scratch_shapes=[
            pltpu.VMEM((256, CHUNK), jnp.bfloat16),
            pltpu.VMEM((256, 256), jnp.float32),
            pltpu.VMEM((256, 1024), jnp.float32),
            pltpu.VMEM((256, 1024), jnp.bfloat16),
        ],
        out_shape=[
            jax.ShapeDtypeStruct((8, 264, LANES), jnp.float32),
            jax.ShapeDtypeStruct((32, 64, LANES), jnp.float32),
        ],
        compiler_params=pltpu.CompilerParams(vmem_limit_bytes=24 * MIB),
        cost_estimate=pl.CostEstimate(
            flops=2 * 256 * 256 * NS, bytes_accessed=12 * MIB, transcendentals=0
        ),
    )(place, *blocks, *panels, near)


def split_kernel(value_ref, out_ref, start):
    out_ref[...] = value_ref[start : start + out_ref.shape[0], :]


def take_rows(value, start):
    rows, cols = value.shape
    return pl.pallas_call(
        functools.partial(split_kernel, start=start),
        out_shape=jax.ShapeDtypeStruct((rows // 2, cols), value.dtype),
        compiler_params=pltpu.CompilerParams(vmem_limit_bytes=3 * MIB),
    )(value)


def pack_kernel(turn_ref, home_ref, out_ref):
    sums = jnp.sum(turn_ref[:, 256:264, :], axis=0)
    for target in range(32):
        row, col = target // 8, target % 8
        out_ref[target, 0:64, :] = home_ref[target, :, :]
        for part in range(8):
            source = ((col // 4) * 4 + part % 4) * 32 + row * 8
            out_ref[target, 64 + part * 8 : 72 + part * 8, :] = turn_ref[
                2 * (col % 4) + part // 4, source : source + 8, :
            ]
        out_ref[target, 128:136, :] = sums


def pack(turn, home):
    return pl.pallas_call(
        pack_kernel,
        out_shape=jax.ShapeDtypeStruct((32, 136, LANES), jnp.float32),
        compiler_params=pltpu.CompilerParams(vmem_limit_bytes=16 * MIB),
        cost_estimate=pl.CostEstimate(flops=0, bytes_accessed=5 * MIB, transcendentals=0),
    )(turn, home)


def finish_kernel(update_ref, totals_ref, own_ref, out_ref, stats_ref):
    totals = jnp.sum(totals_ref[...], axis=0, keepdims=True) * (1.0 / (NS * NS))
    lane = lax.broadcasted_iota(jnp.int32, (1, LANES), 1)
    spread = jnp.sum(jnp.where(lane == 0, totals, 0.0), axis=1, keepdims=True)
    out_ref[...] = update_ref[...] * lax.rsqrt(spread + 1e-06)
    stats_ref[...] = jnp.where(lane == 0, own_ref[0:1, :], jnp.sqrt(totals))


def finish(update, totals, own):
    return pl.pallas_call(
        finish_kernel,
        out_shape=[
            jax.ShapeDtypeStruct(update.shape, jnp.float32),
            jax.ShapeDtypeStruct((1, LANES), jnp.float32),
        ],
        compiler_params=pltpu.CompilerParams(vmem_limit_bytes=16 * MIB),
        cost_estimate=pl.CostEstimate(flops=update.size, bytes_accessed=2 * MIB, transcendentals=0),
    )(update, totals, own)


def update_kernel(tiles_ref, coeff_ref, diag_ref, update_ref, sums_ref, theta_ref):
    totals = jnp.sum(tiles_ref[:, 128:136, :], axis=0)
    lane = lax.broadcasted_iota(jnp.int32, (8, LANES), 1)
    projection = jnp.sum(jnp.where(lane == 0, totals, 0.0))
    weight = jnp.sum(jnp.where(lane == 1, totals, 0.0))
    theta = jnp.full((1, 1), projection) / jnp.full((1, 1), weight)
    squares = jnp.zeros((8, LANES), jnp.float32)
    spread = jnp.zeros((8, LANES), jnp.float32)
    for part in range(2):
        rows = slice(part * LANES, part * LANES + LANES)
        for index in range(8):
            cols = slice(index * LANES, index * LANES + LANES)
            quarter, group = index // 2, index % 2
            at = part * 32 + quarter * 8
            straight = tiles_ref[group * 16 : group * 16 + 16, at : at + 8, :]
            straight = straight.reshape(LANES, LANES).T
            turned = tiles_ref[part * 16 : part * 16 + 16, 64 + index * 8 : 72 + index * 8, :]
            turned = turned.reshape(LANES, LANES)
            coeff = coeff_ref[rows, cols].astype(jnp.float32)
            residual = straight + turned - theta * coeff
            update = residual / jnp.maximum(jnp.abs(diag_ref[rows, cols] - theta), 1.0)
            update_ref[rows, cols] = update
            squares += jnp.sum((residual * residual).reshape(16, 8, LANES), axis=0)
            spread += jnp.sum((update * update).reshape(16, 8, LANES), axis=0)
    theta_ref[...] = jnp.broadcast_to(theta, theta_ref.shape)
    values = jnp.where(lane == 0, jnp.sum(spread), jnp.where(lane == 1, jnp.sum(squares), 0.0))
    sums_ref[...] = jnp.broadcast_to(values[0:1, :], sums_ref.shape)


def make_update(tiles, coeff, diagonal):
    return pl.pallas_call(
        update_kernel,
        out_shape=[
            jax.ShapeDtypeStruct(coeff.shape, jnp.float32),
            jax.ShapeDtypeStruct((256, LANES), jnp.float32),
            jax.ShapeDtypeStruct((8, LANES), jnp.float32),
        ],
        compiler_params=pltpu.CompilerParams(vmem_limit_bytes=16 * MIB),
        cost_estimate=pl.CostEstimate(
            flops=10 * coeff.size, bytes_accessed=5 * MIB, transcendentals=0
        ),
    )(tiles, coeff, diagonal)


def swap(value):
    return lax.ppermute(value, "core", [(0, 1), (1, 0)])


def shift(value, step):
    count = lax.axis_size("z")
    return lax.ppermute(value, "z", [(i, (i + step) % count) for i in range(count)])


def shift_x(value, step):
    def index(x):
        return x % 2 * 2 + x // 2

    pairs = [(index(x), index((x + step) % 4)) for x in range(4)]
    return lax.ppermute(value, ("xlo", "xhi"), pairs)


def exchange(value, axes):
    return lax.all_to_all(value, axes, split_axis=0, concat_axis=0, tiled=True)


def body(ham, coeff, tile_mask, occupation, orbital_energy, coulomb):
    rows, strings = ham.shape
    cols = coeff.shape[1]
    core = lax.axis_index("core")
    xlo = lax.axis_index("xlo")
    z = lax.axis_index("z")
    row_index = (xlo * 8 + z) * 2 + core
    col_index = lax.axis_index("xhi") * 4 + lax.axis_index("y")

    place = jnp.stack([xlo, z, core]).astype(jnp.int32)
    ham, place = lax.optimization_barrier((ham, place))
    pair, pair_mask = swap(ham), swap(tile_mask)
    own_a, own_b = mask_half(ham, tile_mask, 0), mask_half(ham, tile_mask, 1)

    block = exchange(coeff.reshape(32, 8, cols), PLANE)
    block = block.reshape(4, 8, 8, cols).transpose(0, 2, 1, 3).reshape(32, strings)
    block, own_a, own_b, pair, pair_mask = lax.optimization_barrier(
        (block, own_a, own_b, pair, pair_mask)
    )
    far_a, far_b = shift_x(own_a, 1), shift_x(own_b, -1)
    p1, pair, pair_mask = lax.optimization_barrier((shift(block, 1), pair, pair_mask))
    m1 = shift(block, -1)
    pair_a = mask_half(pair, pair_mask, 0)
    p2, pair_a = lax.optimization_barrier((shift(p1, 1), pair_a))
    m2 = shift(m1, -1)
    p3, m3 = shift(p2, 1), shift(m2, -1)
    top, low = take_rows(p3, 0), take_rows(m3, 16)
    top, low, pair, pair_mask = lax.optimization_barrier((top, low, pair, pair_mask))
    pair_b = mask_half(pair, pair_mask, 1)
    top, low, pair_b, far_a, far_b = lax.optimization_barrier(
        (shift(top, 1), shift(low, -1), pair_b, far_a, far_b)
    )
    cross_a, cross_b = swap(far_a), swap(far_b)

    blocks = (block, p1, p2, p3, m1, m2, m3, top, low)
    near = multiply_near(place, blocks, (own_a, own_b, pair_a, pair_b, far_a, far_b))
    turn, home = multiply(place, blocks, (cross_a, cross_b), near)

    turn, home, occupation = lax.optimization_barrier((turn, home, occupation))
    turn = exchange(turn, "z")

    occ_float = occupation.astype(jnp.float32)
    occ_alpha = lax.dynamic_slice_in_dim(occ_float, row_index * rows, rows, 1)
    occ_beta = lax.dynamic_slice_in_dim(occ_float, col_index * cols, cols, 1)
    energy_alpha = jnp.dot(orbital_energy, occ_alpha, precision=lax.Precision.HIGHEST)
    energy_beta = jnp.dot(orbital_energy, occ_beta, precision=lax.Precision.HIGHEST)
    coupling = jnp.dot(
        jnp.dot(occ_alpha.T, coulomb, precision=lax.Precision.HIGHEST),
        occ_beta,
        precision=lax.Precision.HIGHEST,
    )
    diagonal = energy_alpha[:, None] + energy_beta[None, :] + coupling

    turn, diagonal, coeff = lax.optimization_barrier((turn, diagonal, coeff))
    tiles = exchange(pack(turn, home), PLANE)
    update, sums, theta = make_update(tiles, coeff, diagonal)
    correction, stats = finish(update, exchange(sums, AXES), theta)
    return (correction, stats[0, :2])


def solution(mesh):
    fine = Mesh(mesh.devices.reshape(SIZES), AXES)
    in_specs = (P(ROW, None), P(ROW, COL), P(ROW, None), P(), P(), P())
    out_specs = (P(ROW, COL), P())
    return jax.shard_map(body, mesh=fine, in_specs=in_specs, out_specs=out_specs, check_vma=False)
```
